256 devices in a mesh: blk: 8 (over y_lo, x), batch: 32 (over y_hi, z, core).
Axes of the slice: x: 4, y: 4 (y_hi: 2, y_lo: 2; y = y_hi * 2 + y_lo), z: 8, core: 2. Of those that a mesh axis runs over, the one named last changes fastest.
Arguments:
- queries: bfloat16 [32768, 4096], P(('blk', 'batch')), may hold values from -8 to 8
- passages: bfloat16 [32768, 4096], P(('blk', 'batch')), may hold values from -6 to 6
- hard_owner: int32 [32768, 7], P(('blk', 'batch')), may hold values from 0 to 31, as said below
- hard_row: int32 [32768, 7], P(('blk', 'batch')), may hold values from 0 to 127
Outputs:
- losses: float32 [32768], P(('blk', 'batch'))
- query_grad: float32 [32768, 4096], P(('blk', 'batch'))
- passage_grad: float32 [32768, 4096], P(('blk', 'batch'))
The draws below stay inside these ranges and needn't reach their ends.
Inputs may be any that keep to these rules, and one draw needn't show every extreme that they name: `hard_owner`: A query's 7 owners differ. Among the rows of one device no owner is named more than 32 times, and in every blk index one owner is named 32 times by every device of that blk index.
All inputs are finite; a program needn't handle non-finite values.
Results may differ from the reference program's by a relative error of at most 0.00097.
Values may be sent and summed in bfloat16 or wider, within the bound.
No kernel may reach another device: no remote copies, remote signals or barrier semaphores. Data moves between devices by JAX's collectives and lax.ppermute only.
A program may use at most 128 MiB of HBM per device.

```python
import jax
import jax.numpy as jnp
from jax import lax

D = 4096
ROWS = 128
HARD = 7
CYCLE = 8
SHARDS = 32
NQ = 32768
CAP = 32


def hard_lists(key):
    key = jax.random.fold_in(key, 101)
    key_hot, key_blocks, key_rows = jax.random.split(key, 3)
    hot_owner = jax.random.randint(key_hot, (CYCLE,), 0, SHARDS)
    spare_load = HARD * ROWS - CAP
    base_load = spare_load // (SHARDS - 1)
    extra_load = spare_load % (SHARDS - 1)
    swing_max = min(CAP - base_load - 1, base_load)
    pair_count = (SHARDS - 1) // 2

    def one_block(block):
        block_key = jax.random.fold_in(key_blocks, block)
        key_rank, key_swing, key_order = jax.random.split(block_key, 3)
        ranking = jax.random.permutation(key_rank, SHARDS)
        ranking = jnp.where(jnp.arange(SHARDS) == hot_owner[block // SHARDS], -1, ranking)
        owner_order = jnp.argsort(ranking, stable=True).astype(jnp.int32)
        swings = jax.random.randint(key_swing, (pair_count,), 0, swing_max + 1)
        swing_table = jnp.zeros((SHARDS - 1,), jnp.int32)
        swing_table = swing_table.at[0:2 * pair_count:2].set(swings).at[1:2 * pair_count:2].set(-swings)
        other_loads = base_load + (jnp.arange(SHARDS - 1) < extra_load).astype(jnp.int32) + swing_table
        counts = jnp.concatenate([jnp.array([CAP], jnp.int32), other_loads])
        run_ends = jnp.cumsum(counts)
        request = jnp.arange(HARD * ROWS, dtype=jnp.int32)
        run_of = jnp.sum((request[:, None] >= run_ends[None, :]).astype(jnp.int32), axis=1)
        owner_list = owner_order[run_of]
        row_order = jax.random.permutation(key_order, ROWS).astype(jnp.int32)
        owner_table = jnp.zeros((ROWS, HARD), jnp.int32)
        return owner_table.at[row_order[request % ROWS], request // ROWS].set(owner_list)
    owners = jax.vmap(one_block)(jnp.arange(CYCLE * SHARDS)).reshape(NQ, HARD)
    local_rows = jax.random.randint(key_rows, (NQ, HARD), 0, ROWS)
    return (owners, local_rows)


def passage_table(key, row_low):
    key = jax.random.fold_in(key, 202)
    key_base, key_scale = jax.random.split(key, 2)
    values = jax.random.truncated_normal(key_base, -6.0, 6.0, (NQ, D))
    values = values * row_low ** jax.random.uniform(key_scale, (NQ, 1))
    planted_rows = jnp.array([((CYCLE - 1) * SHARDS + group) * ROWS + second for group in range(3) for second in range(2)], jnp.int32)
    return values.at[planted_rows].set(values[planted_rows])


def query_table(key, values, owners, local_rows):
    key = jax.random.fold_in(key, 303)
    key_base = jax.random.fold_in(key, 0)
    result = jax.random.truncated_normal(key_base, -6.0, 6.0, (NQ, D)) + 0.094 * values
    cycle_of = jnp.arange(NQ, dtype=jnp.int32) // (SHARDS * ROWS)
    for column in range(HARD):
        gather_index = (cycle_of * SHARDS + owners[:, column]) * ROWS + local_rows[:, column]
        result = result + 0.078 * values[gather_index]
    planted_rows = jnp.array([group * ROWS for group in range(3)], jnp.int32)
    result = result.at[planted_rows].set(result[planted_rows])
    return jnp.clip(result, -8.0, 8.0)


def draw_hard_owner(key, part):
    owners, local_rows = hard_lists(key)
    return owners


def draw_hard_row(key, part):
    owners, local_rows = hard_lists(key)
    return local_rows


def draw_passages(key, part):
    values = passage_table(key, 1.0)
    return values.astype(jnp.bfloat16)


def draw_queries(key, part):
    owners, local_rows = hard_lists(key)
    values = passage_table(key, 1.0)
    result = query_table(key, values, owners, local_rows)
    return result.astype(jnp.bfloat16)


def setup_inputs(seed: int = 0) -> dict:
    splits = jax.random.split(jax.random.key(seed), 5)
    return {
        "queries": draw_queries(jax.random.fold_in(splits[4], 71), 0),
        "passages": draw_passages(jax.random.fold_in(splits[4], 71), 0),
        "hard_owner": draw_hard_owner(jax.random.fold_in(splits[4], 71), 0),
        "hard_row": draw_hard_row(jax.random.fold_in(splits[4], 71), 0),
    }


def group_terms(packed):
    query_group, passage_group, hard_group = packed
    logit_scale = D ** -0.5
    scores = jnp.dot(query_group, passage_group.T, preferred_element_type=jnp.float32) * logit_scale
    row_max = jnp.maximum(jnp.max(scores, axis=1), jnp.max(hard_group, axis=1))
    summed = jnp.sum(jnp.exp(scores - row_max[:, None]), axis=1) + jnp.sum(jnp.exp(hard_group - row_max[:, None]), axis=1)
    log_total = row_max + jnp.log(summed)
    weights = jnp.exp(scores - log_total[:, None]).astype(jnp.bfloat16)
    query_part = jnp.dot(weights, passage_group, preferred_element_type=jnp.float32)
    passage_part = jnp.dot(weights.T, query_group, preferred_element_type=jnp.float32)
    return log_total, jnp.diagonal(scores), query_part, passage_part


def regroup(values):
    shaped = values.reshape((SHARDS, CYCLE, ROWS) + values.shape[2:])
    return jnp.swapaxes(shaped, 0, 1)


def reference(queries, passages, hard_owner, hard_row):
    logit_scale = D ** -0.5
    query_blocks = queries.reshape(CYCLE, SHARDS, ROWS, D)
    passage_blocks = passages.reshape(CYCLE, SHARDS, ROWS, D)
    owner_ids = hard_owner.reshape(CYCLE, SHARDS, ROWS, HARD)
    row_ids = hard_row.reshape(CYCLE, SHARDS, ROWS, HARD)
    cycle_index = jnp.broadcast_to(jnp.arange(CYCLE, dtype=jnp.int32)[:, None, None], (CYCLE, SHARDS, ROWS))
    query_float = query_blocks.astype(jnp.float32)
    hard_list = []
    for column in range(HARD):
        picked = passage_blocks[cycle_index, owner_ids[..., column], row_ids[..., column]].astype(jnp.float32)
        hard_list.append(jnp.sum(query_float * picked, axis=-1) * logit_scale)
    hard_scores = jnp.stack(hard_list, axis=-1)
    query_groups = jnp.swapaxes(query_blocks, 0, 1).reshape(SHARDS, CYCLE * ROWS, D)
    passage_groups = jnp.swapaxes(passage_blocks, 0, 1).reshape(SHARDS, CYCLE * ROWS, D)
    hard_groups = jnp.swapaxes(hard_scores, 0, 1).reshape(SHARDS, CYCLE * ROWS, HARD)
    log_total, positive, query_part, passage_part = lax.map(group_terms, (query_groups, passage_groups, hard_groups))
    log_total = regroup(log_total)
    losses = log_total - regroup(positive)
    query_grad = regroup(query_part) - passage_blocks.astype(jnp.float32)
    passage_grad = regroup(passage_part) - query_float
    for column in range(HARD):
        picked = passage_blocks[cycle_index, owner_ids[..., column], row_ids[..., column]].astype(jnp.float32)
        rounded = lax.optimization_barrier(jnp.exp(hard_scores[..., column] - log_total).astype(jnp.bfloat16))
        hard_weight = rounded.astype(jnp.float32)[..., None]
        query_grad = query_grad + hard_weight * picked
        passage_grad = passage_grad.at[cycle_index, owner_ids[..., column], row_ids[..., column]].add(hard_weight * query_float)
    return losses.reshape(NQ), query_grad.reshape(NQ, D), passage_grad.reshape(NQ, D)
```

```python
import functools

import jax
import jax.numpy as jnp
from jax import lax
from jax.experimental import pallas as pl
from jax.experimental.pallas import tpu as pltpu
from jax.sharding import PartitionSpec as P

ROWS = 128
WIDTH = 4096
HARD = 7
SCALE = WIDTH ** (-0.5)
AXES = ("blk", "batch")
VMEM_LIMIT = 40 * 1024 * 1024
F32, BF16, I32, I16 = jnp.float32, jnp.bfloat16, jnp.int32, jnp.int16


def _pairs(move):
    pairs = []
    for i in range(256):
        a, b = divmod(i, 32)
        yl, x = divmod(a, 4)
        yh, rest = divmod(b, 16)
        z, c = divmod(rest, 2)
        yl, x, yh, z, c = move(yl, x, yh, z, c)
        pairs.append((i, (yl * 4 + x) * 32 + yh * 16 + z * 2 + c))
    return pairs


def _x(d):
    return _pairs(lambda yl, x, yh, z, c: (yl, (x + d) % 4, yh, z, c))


def _z(d):
    return _pairs(lambda yl, x, yh, z, c: (yl, x, yh, (z + d) % 8, c))


def _zxor(m):
    return _pairs(lambda yl, x, yh, z, c: (yl, x, yh, z ^ m, c))


SWAP_CORE = _pairs(lambda yl, x, yh, z, c: (yl, x, yh, z, 1 - c))
SWAP_YH = _pairs(lambda yl, x, yh, z, c: (yl, x, 1 - yh, z, c))
SWAP_YL = _pairs(lambda yl, x, yh, z, c: (1 - yl, x, yh, z, c))
OFFSETS = (0, -1, 1, -2, 2, -3, 3, 4)


def send(value, pairs):
    return lax.ppermute(value, AXES, pairs)


def z_gather(v):
    f, g = [v], [v]
    for _ in range(3):
        f.append(send(f[-1], _z(1)))
        g.append(send(g[-1], _z(-1)))
    half = ROWS // 2
    top = send(f[3][:half], _z(1))
    bottom = send(g[3][half:], _z(-1))
    return [v, f[1], g[1], f[2], g[2], f[3], g[3], top, bottom]


def x_gather(v):
    w = send(v, SWAP_YL)
    f, g = send(v, _x(1)), send(v, _x(-1))
    wf, wg = send(w, _x(1)), send(w, _x(-1))
    return [v, f, g, send(f, _x(1)), w, wf, wg, send(wg, _x(-1))]


def x_gather_row(row):
    pair = jnp.concatenate([row, send(row, SWAP_YL)], axis=0)
    parts = [pair, send(pair, _x(1)), send(pair, _x(-1)), send(pair, _x(2))]
    return jnp.stack(parts, axis=1).reshape(1, 8 * ROWS)


def z_gather_xor(v):
    v = v[None]
    for m in (1, 2, 4):
        v = jnp.concatenate([v, send(v, _zxor(m))], axis=0)
    return v


def params(**kw):
    return pltpu.CompilerParams(vmem_limit_bytes=VMEM_LIMIT, **kw)


def cost(flops, nbytes):
    return pl.CostEstimate(flops=flops, bytes_accessed=nbytes, transcendentals=0)


def cat(refs):
    return jnp.concatenate([r[...] for r in refs], axis=0)


def nt(l, r):
    return lax.dot_general(l, r, (((1,), (1,)), ((), ())), preferred_element_type=F32)


def whole(shape):
    return pl.BlockSpec(shape, lambda k: tuple(0 for _ in shape))


SMEM_SPEC = pl.BlockSpec(memory_space=pltpu.SMEM)


def col_specs(arrays, chunk):
    return [pl.BlockSpec((a.shape[0], chunk), lambda k: (0, k)) for a in arrays]


def rows_of(arrays):
    return sum(a.shape[0] for a in arrays)


def scores(lhs, rhs, chunk=1024):
    m, n, nl = rows_of(lhs), rows_of(rhs), len(lhs)

    def kernel(*refs):
        out = refs[-1]
        d = nt(cat(refs[:nl]), cat(refs[nl:-1]))
        k = pl.program_id(0)

        @pl.when(k == 0)
        def _():
            out[...] = d

        @pl.when(k > 0)
        def _():
            out[...] += d

    return pl.pallas_call(
        kernel,
        grid=(WIDTH // chunk,),
        in_specs=col_specs(lhs + rhs, chunk),
        out_specs=whole((m, n)),
        out_shape=jax.ShapeDtypeStruct((m, n), F32),
        compiler_params=params(),
        cost_estimate=cost(2 * m * n * WIDTH, 2 * (m + n) * WIDTH + 4 * m * n),
        name="scores",
    )(*lhs, *rhs)


def hard_scores(bases, ids, line, group, chunk=512):
    m, n, nl = rows_of(line), rows_of(group), len(line)
    steps = WIDTH // chunk

    def kernel(base, ids_ref, *refs):
        out, acc = refs[-2], refs[-1]
        d = nt(cat(refs[:nl]), cat(refs[nl:-2]))
        k = pl.program_id(0)

        @pl.when(k == 0)
        def _():
            acc[...] = d

        @pl.when(k > 0)
        def _():
            acc[...] += d

        @pl.when(k == steps - 1)
        def _():
            iota = lax.broadcasted_iota(I32, (ROWS, ROWS), 0)
            for g in range(n // ROWS):
                cols = slice(g * ROWS, (g + 1) * ROWS)
                idg = ids_ref[:, cols]
                sums = [jnp.zeros((1, ROWS), F32) for _ in range(HARD)]
                for i in range(m // ROWS):
                    rel = idg - base[i]
                    s = acc[i * ROWS:(i + 1) * ROWS, cols]
                    for j in range(HARD):
                        hit = jnp.where(iota == rel[j:j + 1], s, 0.0)
                        sums[j] += jnp.sum(hit, axis=0, keepdims=True)
                out[:, cols] = jnp.concatenate(sums + [jnp.zeros((1, ROWS), F32)], axis=0)

    return pl.pallas_call(
        kernel,
        grid=(steps,),
        in_specs=[SMEM_SPEC, whole((8, n))] + col_specs(line + group, chunk),
        out_specs=whole((8, n)),
        out_shape=jax.ShapeDtypeStruct((8, n), F32),
        scratch_shapes=[pltpu.VMEM((m, n), F32)],
        compiler_params=params(),
        cost_estimate=cost(2 * m * n * WIDTH, 2 * (m + n) * WIDTH),
        name="hard_scores",
    )(bases, ids, *line, *group)


def softmax(st, hs):
    m = st.shape[0]

    def kernel(st_ref, hs_ref, lt_ref, loss_ref, w_ref, hw_ref):
        s = st_ref[...] * SCALE
        real = lax.broadcasted_iota(I32, (8, ROWS), 0) < HARD
        h = jnp.where(real, hs_ref[...] * SCALE, -jnp.inf)
        t = jnp.maximum(
            jnp.max(s, axis=0, keepdims=True), jnp.max(h, axis=0, keepdims=True)
        )
        total = jnp.sum(jnp.exp(s - t), axis=0, keepdims=True) + jnp.sum(
            jnp.exp(h - t), axis=0, keepdims=True
        )
        lt = t + jnp.log(total)
        lt_ref[...] = lt
        own = s[:ROWS]
        i0 = lax.broadcasted_iota(I32, (ROWS, ROWS), 0)
        i1 = lax.broadcasted_iota(I32, (ROWS, ROWS), 1)
        loss_ref[...] = lt - jnp.sum(jnp.where(i0 == i1, own, 0.0), axis=0, keepdims=True)
        w = jnp.exp(s - lt)
        for i in range(m // ROWS):
            w_ref[:, i * ROWS:(i + 1) * ROWS] = w[i * ROWS:(i + 1) * ROWS].T.astype(BF16)
        hw = jnp.exp(h - lt).astype(BF16).astype(F32)
        hw_ref[...] = jnp.where(real, hw, 0.0)

    row = jax.ShapeDtypeStruct((1, ROWS), F32)
    return pl.pallas_call(
        kernel,
        out_shape=[
            row,
            row,
            jax.ShapeDtypeStruct((ROWS, m), BF16),
            jax.ShapeDtypeStruct((8, ROWS), F32),
        ],
        compiler_params=params(),
        cost_estimate=cost(10 * m * ROWS, 6 * m * ROWS),
        name="softmax",
    )(st, hs)


def spread_tile(ids, hw, base):
    rel = ids - base
    iota = lax.broadcasted_iota(I32, (ROWS, ROWS), 0)
    tile = jnp.zeros((ROWS, ROWS), F32)
    for j in range(HARD):
        tile = jnp.where(iota == rel[j:j + 1], hw[j:j + 1], tile)
    return tile


def fill_forward(w, line_base, ids, hw, groups):
    for g in range(groups):
        cols = slice(g * ROWS, (g + 1) * ROWS)
        for i in range(8):
            tile = spread_tile(ids[:, cols], hw[:, cols], line_base[i])
            w[cols, i * ROWS:(i + 1) * ROWS] = tile.T.astype(BF16)


def fill_backward(w, group_base, order, first, ids, hw, groups):
    for i in range(8):
        ids_i, hw_i = ids[order[i]], hw[order[i]]
        for g in range(groups):
            tile = spread_tile(ids_i, hw_i, group_base[first + g])
            w[g * ROWS:(g + 1) * ROWS, i * ROWS:(i + 1) * ROWS] = tile.astype(BF16)


def far_grad(fill, small, small_specs, line, chunk=512):
    ns, nl = len(small), len(line)

    def kernel(*refs):
        sm, ln = refs[:ns], refs[ns:ns + nl]
        out0, out1, w = refs[ns + nl:]

        @pl.when(pl.program_id(0) == 0)
        def _():
            fill(w, *sm, groups=2)

        d = jnp.dot(w[...], cat(ln), preferred_element_type=F32)
        out0[...] = d[:ROWS]
        out1[...] = d[ROWS:]

    out = jax.ShapeDtypeStruct((ROWS, WIDTH), F32)
    return pl.pallas_call(
        kernel,
        grid=(WIDTH // chunk,),
        in_specs=small_specs + col_specs(line, chunk),
        out_specs=col_specs([out, out], chunk),
        out_shape=[out, out],
        scratch_shapes=[pltpu.VMEM((2 * ROWS, 8 * ROWS), BF16)],
        compiler_params=params(),
        cost_estimate=cost(4 * ROWS * 8 * ROWS * WIDTH, 12 * ROWS * 2 * WIDTH),
        name="far_grad",
    )(*small, *line)


def near_grad(fill, small, small_specs, line, w_in, block, minus, chunk=512):
    ns, nl, nb = len(small), len(line), len(block)

    def kernel(*refs):
        sm, ln = refs[:ns], refs[ns:ns + nl]
        w_ref, bl = refs[ns + nl], refs[ns + nl + 1:ns + nl + 1 + nb]
        minus_ref, out0, out1, w = refs[ns + nl + 1 + nb:]

        @pl.when(pl.program_id(0) == 0)
        def _():
            fill(w, *sm, groups=2)

        d = jnp.dot(w[...], cat(ln), preferred_element_type=F32)
        e = jnp.dot(w_ref[...], cat(bl), preferred_element_type=F32)
        out0[...] = d[:ROWS] + e - minus_ref[...].astype(F32)
        out1[...] = d[ROWS:]

    out = jax.ShapeDtypeStruct((ROWS, WIDTH), F32)
    return pl.pallas_call(
        kernel,
        grid=(WIDTH // chunk,),
        in_specs=small_specs
        + col_specs(line, chunk)
        + [whole(w_in.shape)]
        + col_specs(block + [minus], chunk),
        out_specs=col_specs([out, out], chunk),
        out_shape=[out, out],
        scratch_shapes=[pltpu.VMEM((2 * ROWS, 8 * ROWS), BF16)],
        compiler_params=params(),
        cost_estimate=cost(6 * ROWS * 8 * ROWS * WIDTH, 22 * ROWS * 2 * WIDTH),
        name="near_grad",
    )(*small, *line, w_in, *block, minus)


def quantize(a, b):
    def kernel(a_ref, b_ref, out):
        v = a_ref[...] + b_ref[...]
        top = jnp.max(jnp.abs(v), axis=1, keepdims=True)
        e = jnp.ceil(jnp.log2(jnp.maximum(top, 1e-30) / 32000.0))
        out[:, :WIDTH] = jnp.round(v * jnp.exp2(-e)).astype(I32).astype(I16)
        out[:, WIDTH:] = jnp.broadcast_to(e, (ROWS, 128)).astype(I32).astype(I16)

    return pl.pallas_call(
        kernel,
        out_shape=jax.ShapeDtypeStruct((ROWS, WIDTH + 128), I16),
        compiler_params=params(),
        cost_estimate=cost(6 * ROWS * WIDTH, 10 * ROWS * WIDTH),
        name="quantize",
    )(a, b)


def dequantize(coded):
    step = jnp.exp2(coded[:, WIDTH:WIDTH + 1].astype(F32))
    return coded[:, :WIDTH].astype(F32) * step


def back_weights(p, block, lt_row, chunk=1024):
    nb = len(block)
    n = rows_of(block)
    steps = WIDTH // chunk

    def kernel(p_ref, lt_ref, *refs):
        out, acc = refs[-2], refs[-1]
        d = nt(p_ref[...], cat(refs[:nb]))
        k = pl.program_id(0)

        @pl.when(k == 0)
        def _():
            acc[...] = d

        @pl.when(k > 0)
        def _():
            acc[...] += d

        @pl.when(k == steps - 1)
        def _():
            out[...] = jnp.exp(acc[...] * SCALE - lt_ref[...]).astype(BF16)

    return pl.pallas_call(
        kernel,
        grid=(steps,),
        in_specs=col_specs([p], chunk) + [whole((1, n))] + col_specs(block, chunk),
        out_specs=whole((ROWS, n)),
        out_shape=jax.ShapeDtypeStruct((ROWS, n), BF16),
        scratch_shapes=[pltpu.VMEM((ROWS, n), F32)],
        compiler_params=params(),
        cost_estimate=cost(2 * ROWS * n * WIDTH, 2 * (ROWS + n) * WIDTH),
        name="back_weights",
    )(p, lt_row, *block)


def body(q, p, hard_owner, hard_row):
    b = lax.axis_index("batch").astype(I32)
    z = (b // 2) % 8
    line_z = (z + jnp.array(OFFSETS, I32)) % 8
    order = z ^ line_z
    line_base = ((b // 16) * 16 + line_z * 2 + b % 2) * ROWS
    group_base = (b ^ jnp.array([0, 1, 16, 17], I32)) * ROWS

    ids = (hard_owner * ROWS + hard_row).T
    ids = jnp.concatenate([ids, jnp.full((1, ROWS), -1, I32)], axis=0)
    ids_near = jnp.concatenate([ids, send(ids, SWAP_CORE)], axis=1)
    ids_far = send(ids_near, SWAP_YH)
    ids_group = jnp.concatenate([ids_near, ids_far], axis=1)
    ids_line = z_gather_xor(ids)

    q_y = send(q, SWAP_YH)
    q_group = [q, send(q, SWAP_CORE), q_y, send(q_y, SWAP_CORE)]
    p_line = z_gather(p)
    p_block = x_gather(p)

    st = scores(p_block, [q])
    hs = hard_scores(line_base, ids_group, p_line, q_group)
    hs = hs.reshape(8, 2, 2, ROWS)
    mine = hs[:, :, 0] + send(hs[:, :, 1], SWAP_CORE)
    hs = mine[:, 0] + send(mine[:, 1], SWAP_YH)
    lt, loss, w_in, hw = softmax(st, hs)

    hw_near = jnp.concatenate([hw, send(hw, SWAP_CORE)], axis=1)
    hw_far = send(hw_near, SWAP_YH)
    hw_line = z_gather_xor(hw)
    lt_row = x_gather_row(lt)

    q_line = z_gather(q)
    q_block = x_gather(q)

    small8 = [whole((8, 2 * ROWS))] * 2
    h_y, h_yc = far_grad(
        fill_forward, [line_base, ids_far, hw_far], [SMEM_SPEC] + small8, p_line
    )
    far = send(quantize(h_y, send(h_yc, SWAP_CORE)), SWAP_YH)
    part, h_c = near_grad(
        fill_forward,
        [line_base, ids_near, hw_near],
        [SMEM_SPEC] + small8,
        p_line,
        w_in,
        p_block,
        p,
    )
    query_grad = part + send(h_c, SWAP_CORE) + dequantize(far)

    w_back = back_weights(p, q_block, lt_row)
    line_specs = [SMEM_SPEC, SMEM_SPEC, whole((8, 8, ROWS)), whole((8, 8, ROWS))]

    def fill(first):
        def run(w, base, order_ref, ids_ref, hw_ref, groups):
            fill_backward(w, base, order_ref, first, ids_ref, hw_ref, groups)

        return run

    small = [group_base, order, ids_line, hw_line]
    h_y, h_yc = far_grad(fill(2), small, line_specs, q_line)
    far = send(quantize(h_y, send(h_yc, SWAP_CORE)), SWAP_YH)
    part, h_c = near_grad(fill(0), small, line_specs, q_line, w_back, q_block, q)
    passage_grad = part + send(h_c, SWAP_CORE) + dequantize(far)
    return loss.reshape(ROWS), query_grad, passage_grad


def solution(mesh):
    rows = P(("blk", "batch"), None)
    return jax.shard_map(
        body,
        mesh=mesh,
        in_specs=(rows, rows, rows, rows),
        out_specs=(P(("blk", "batch")), rows, rows),
        check_vma=False,
    )
```

```python
import functools

import jax
import jax.numpy as jnp
from jax import lax
from jax.experimental import pallas as pl
from jax.experimental.pallas import tpu as pltpu
from jax.sharding import PartitionSpec as P

ROWS = 128
WIDTH = 4096
HARD = 7
SCALE = WIDTH ** (-0.5)
AXES = ("blk", "batch")
VMEM_LIMIT = 16 * 1024 * 1024
F32, BF16, I32, I16 = jnp.float32, jnp.bfloat16, jnp.int32, jnp.int16


def _pairs(move):
    pairs = []
    for i in range(256):
        a, b = divmod(i, 32)
        yl, x = divmod(a, 4)
        yh, rest = divmod(b, 16)
        z, c = divmod(rest, 2)
        yl, x, yh, z, c = move(yl, x, yh, z, c)
        pairs.append((i, (yl * 4 + x) * 32 + yh * 16 + z * 2 + c))
    return pairs


def _x(d):
    return _pairs(lambda yl, x, yh, z, c: (yl, (x + d) % 4, yh, z, c))


def _z(d):
    return _pairs(lambda yl, x, yh, z, c: (yl, x, yh, (z + d) % 8, c))


def _zxor(m):
    return _pairs(lambda yl, x, yh, z, c: (yl, x, yh, z ^ m, c))


SWAP_CORE = _pairs(lambda yl, x, yh, z, c: (yl, x, yh, z, 1 - c))
SWAP_YH = _pairs(lambda yl, x, yh, z, c: (yl, x, 1 - yh, z, c))
SWAP_YL = _pairs(lambda yl, x, yh, z, c: (1 - yl, x, yh, z, c))
OFFSETS = (0, -1, 1, -2, 2, -3, 3, 4)


def send(value, pairs):
    return lax.ppermute(value, AXES, pairs)


def tie(*values):
    return lax.optimization_barrier(values)


def params(**kw):
    return pltpu.CompilerParams(vmem_limit_bytes=VMEM_LIMIT, **kw)


def cost(flops, nbytes):
    return pl.CostEstimate(flops=flops, bytes_accessed=nbytes, transcendentals=0)


def cat(refs):
    return jnp.concatenate([r[...] for r in refs], axis=0)


def nt(l, r):
    return lax.dot_general(l, r, (((1,), (1,)), ((), ())), preferred_element_type=F32)


def whole(shape):
    return pl.BlockSpec(shape, lambda k: tuple(0 for _ in shape))


SMEM_SPEC = pl.BlockSpec(memory_space=pltpu.SMEM)


def col_specs(arrays, chunk):
    return [pl.BlockSpec((a.shape[0], chunk), lambda k: (0, k)) for a in arrays]


def rows_of(arrays):
    return sum(a.shape[0] for a in arrays)


def scores(lhs, rhs, chunk=1024):
    m, n, nl = rows_of(lhs), rows_of(rhs), len(lhs)

    def kernel(*refs):
        out = refs[-1]
        d = nt(cat(refs[:nl]), cat(refs[nl:-1]))
        k = pl.program_id(0)

        @pl.when(k == 0)
        def _():
            out[...] = d

        @pl.when(k > 0)
        def _():
            out[...] += d

    return pl.pallas_call(
        kernel,
        grid=(WIDTH // chunk,),
        in_specs=col_specs(lhs + rhs, chunk),
        out_specs=whole((m, n)),
        out_shape=jax.ShapeDtypeStruct((m, n), F32),
        compiler_params=params(),
        cost_estimate=cost(2 * m * n * WIDTH, 2 * (m + n) * WIDTH + 4 * m * n),
        name="scores",
    )(*lhs, *rhs)


def hard_scores(bases, which, ids, line, group, chunk=1024):
    m, n, nl = rows_of(line), rows_of(group), len(line)
    steps = WIDTH // chunk

    def kernel(base, ids_ref, *refs):
        out, acc = refs[-2], refs[-1]
        d = nt(cat(refs[:nl]), cat(refs[nl:-2]))
        k = pl.program_id(0)

        @pl.when(k == 0)
        def _():
            acc[...] = d

        @pl.when(k > 0)
        def _():
            acc[...] += d

        @pl.when(k == steps - 1)
        def _():
            iota = lax.broadcasted_iota(I32, (ROWS, ROWS), 0)
            for g in range(n // ROWS):
                cols = slice(g * ROWS, (g + 1) * ROWS)
                idg = ids_ref[:, cols]
                sums = [jnp.zeros((1, ROWS), F32) for _ in range(HARD)]
                for i in range(m // ROWS):
                    rel = idg - base[which[i]]
                    s = acc[i * ROWS:(i + 1) * ROWS, cols]
                    for j in range(HARD):
                        hit = jnp.where(iota == rel[j:j + 1], s, 0.0)
                        sums[j] += jnp.sum(hit, axis=0, keepdims=True)
                out[:, cols] = jnp.concatenate(sums + [jnp.zeros((1, ROWS), F32)], axis=0)

    return pl.pallas_call(
        kernel,
        grid=(steps,),
        in_specs=[SMEM_SPEC, whole((8, n))] + col_specs(line + group, chunk),
        out_specs=whole((8, n)),
        out_shape=jax.ShapeDtypeStruct((8, n), F32),
        scratch_shapes=[pltpu.VMEM((m, n), F32)],
        compiler_params=params(),
        cost_estimate=cost(2 * m * n * WIDTH, 2 * (m + n) * WIDTH),
        name="hard_scores",
    )(bases, ids, *line, *group)


def softmax(st, hs, ids):
    m = st.shape[0]

    def kernel(st_ref, hs_ref, ids_ref, lt_ref, loss_ref, w_ref, pack_ref):
        s = st_ref[...] * SCALE
        real = lax.broadcasted_iota(I32, (8, ROWS), 0) < HARD
        h = jnp.where(real, hs_ref[...] * SCALE, -jnp.inf)
        t = jnp.maximum(
            jnp.max(s, axis=0, keepdims=True), jnp.max(h, axis=0, keepdims=True)
        )
        total = jnp.sum(jnp.exp(s - t), axis=0, keepdims=True) + jnp.sum(
            jnp.exp(h - t), axis=0, keepdims=True
        )
        lt = t + jnp.log(total)
        lt_ref[...] = lt
        own = s[:ROWS]
        i0 = lax.broadcasted_iota(I32, (ROWS, ROWS), 0)
        i1 = lax.broadcasted_iota(I32, (ROWS, ROWS), 1)
        loss_ref[...] = lt - jnp.sum(jnp.where(i0 == i1, own, 0.0), axis=0, keepdims=True)
        w = jnp.exp(s - lt)
        for i in range(m // ROWS):
            w_ref[:, i * ROWS:(i + 1) * ROWS] = w[i * ROWS:(i + 1) * ROWS].T.astype(BF16)
        hw = jnp.exp(h - lt).astype(BF16).astype(F32)
        pack_ref[:8] = jnp.where(real, hw, jnp.broadcast_to(lt, (8, ROWS)))
        pack_ref[8:] = ids_ref[...].astype(F32)

    row = jax.ShapeDtypeStruct((1, ROWS), F32)
    return pl.pallas_call(
        kernel,
        out_shape=[
            row,
            row,
            jax.ShapeDtypeStruct((ROWS, m), BF16),
            jax.ShapeDtypeStruct((16, ROWS), F32),
        ],
        compiler_params=params(),
        cost_estimate=cost(10 * m * ROWS, 6 * m * ROWS),
        name="softmax",
    )(st, hs, ids)


def spread_tile(pack, base):
    hw, rel = pack[:8], pack[8:].astype(I32) - base
    iota = lax.broadcasted_iota(I32, (ROWS, ROWS), 0)
    tile = jnp.zeros((ROWS, ROWS), F32)
    for j in range(HARD):
        tile = jnp.where(iota == rel[j:j + 1], hw[j:j + 1], tile)
    return tile


def fill_forward(w, line_base, packs, groups):
    for g in range(groups):
        cols = slice(g * ROWS, (g + 1) * ROWS)
        for i in range(8):
            tile = spread_tile(packs[:, cols], line_base[i])
            w[cols, i * ROWS:(i + 1) * ROWS] = tile.T.astype(BF16)


def fill_backward(w, group_base, order, packs, first, which, groups):
    for i, block in enumerate(which):
        pack = packs[order[block]]
        for g in range(groups):
            tile = spread_tile(pack, group_base[first + g])
            w[g * ROWS:(g + 1) * ROWS, i * ROWS:(i + 1) * ROWS] = tile.astype(BF16)


def hard_grad(fill, small, small_specs, line, groups, chunk=512):
    ns, nl = len(small), len(line)
    depth = rows_of(line)

    def kernel(*refs):
        sm, ln = refs[:ns], refs[ns:ns + nl]
        outs, w = refs[ns + nl:-1], refs[-1]

        @pl.when(pl.program_id(0) == 0)
        def _():
            fill(w, *sm, groups=groups)

        d = jnp.dot(w[...], cat(ln), preferred_element_type=F32)
        for g in range(groups):
            outs[g][...] = d[g * ROWS:(g + 1) * ROWS]

    out = [jax.ShapeDtypeStruct((ROWS, WIDTH), F32)] * groups
    return pl.pallas_call(
        kernel,
        grid=(WIDTH // chunk,),
        in_specs=small_specs + col_specs(line, chunk),
        out_specs=col_specs(out, chunk),
        out_shape=out,
        scratch_shapes=[pltpu.VMEM((groups * ROWS, depth), BF16)],
        compiler_params=params(),
        cost_estimate=cost(
            2 * groups * ROWS * depth * WIDTH, 2 * (depth + 2 * groups * ROWS) * WIDTH
        ),
        name="hard_grad",
    )(*small, *line)


def encode(v, out):
    top = jnp.max(jnp.abs(v), axis=1, keepdims=True)
    e = jnp.ceil(jnp.log2(jnp.maximum(top, 1e-30) / 32000.0))
    out[:, :WIDTH] = jnp.round(v * jnp.exp2(-e)).astype(I32).astype(I16)
    out[:, WIDTH:] = jnp.broadcast_to(e, (v.shape[0], 128)).astype(I32).astype(I16)


def last_far(fill, small, small_specs, line, before, chunk=512):
    ns, nl = len(small), len(line)
    depth = rows_of(line)
    steps = WIDTH // chunk

    def kernel(*refs):
        sm, ln = refs[:ns], refs[ns:ns + nl]
        b0, b1, out, w, total = refs[ns + nl:]
        k = pl.program_id(0)

        @pl.when(k == 0)
        def _():
            fill(w, *sm)

        d = jnp.dot(w[...], cat(ln), preferred_element_type=F32)
        cols = pl.ds(pl.multiple_of(k * chunk, chunk), chunk)
        total[:, cols] = d + b0[...] + b1[...]

        @pl.when(k == steps - 1)
        def _():
            encode(total[...], out)

    return pl.pallas_call(
        kernel,
        grid=(steps,),
        in_specs=small_specs + col_specs(line, chunk) + col_specs(list(before), chunk),
        out_specs=whole((ROWS, WIDTH + 128)),
        out_shape=jax.ShapeDtypeStruct((ROWS, WIDTH + 128), I16),
        scratch_shapes=[pltpu.VMEM((ROWS, depth), BF16), pltpu.VMEM((ROWS, WIDTH), F32)],
        compiler_params=params(),
        cost_estimate=cost(2 * ROWS * depth * WIDTH, 2 * (depth + 5 * ROWS) * WIDTH),
        name="last_far",
    )(*small, *line, *before)


def near_grad(fill, small, small_specs, line, w_in, block, minus, groups, came=(), chunk=512):
    ns, nl, nb, nc = len(small), len(line), len(block), len(came)
    depth = rows_of(line)

    def kernel(*refs):
        sm, ln = refs[:ns], refs[ns:ns + nl]
        w_ref, bl = refs[ns + nl], refs[ns + nl + 1:ns + nl + 1 + nb]
        minus_ref, *rest = refs[ns + nl + 1 + nb:]
        cm, outs, w = rest[:nc], rest[nc:-1], rest[-1]

        @pl.when(pl.program_id(0) == 0)
        def _():
            fill(w, *sm, groups=groups)

        d = jnp.dot(w[...], cat(ln), preferred_element_type=F32)
        e = jnp.dot(w_ref[...], cat(bl), preferred_element_type=F32)
        own = d[:ROWS] + e - minus_ref[...].astype(F32)
        for c in cm:
            own += c[...]
        outs[0][...] = own
        for g in range(1, groups):
            outs[g][...] = d[g * ROWS:(g + 1) * ROWS]

    out = [jax.ShapeDtypeStruct((ROWS, WIDTH), F32)] * groups
    return pl.pallas_call(
        kernel,
        grid=(WIDTH // chunk,),
        in_specs=small_specs
        + col_specs(line, chunk)
        + [whole(w_in.shape)]
        + col_specs(block + [minus] + list(came), chunk),
        out_specs=col_specs(out, chunk),
        out_shape=out,
        scratch_shapes=[pltpu.VMEM((groups * ROWS, depth), BF16)],
        compiler_params=params(),
        cost_estimate=cost(6 * ROWS * 8 * ROWS * WIDTH, 22 * ROWS * 2 * WIDTH),
        name="near_grad",
    )(*small, *line, w_in, *block, minus, *came)


def quantize(a, b):
    half = ROWS // 2

    def kernel(a_ref, b_ref, out0, out1):
        encode(a_ref[:half] + b_ref[:half], out0)
        encode(a_ref[half:] + b_ref[half:], out1)

    out = jax.ShapeDtypeStruct((half, WIDTH + 128), I16)
    return pl.pallas_call(
        kernel,
        out_shape=[out, out],
        compiler_params=params(),
        cost_estimate=cost(6 * ROWS * WIDTH, 10 * ROWS * WIDTH),
        name="quantize",
    )(a, b)


def dequantize(coded):
    step = jnp.exp2(coded[:, WIDTH:WIDTH + 1].astype(F32))
    return coded[:, :WIDTH].astype(F32) * step


def back_weights(p, block, lt_row, chunk=1024):
    nb = len(block)
    n = rows_of(block)
    steps = WIDTH // chunk

    def kernel(p_ref, lt_ref, *refs):
        out, acc = refs[-2], refs[-1]
        d = nt(p_ref[...], cat(refs[:nb]))
        k = pl.program_id(0)

        @pl.when(k == 0)
        def _():
            acc[...] = d

        @pl.when(k > 0)
        def _():
            acc[...] += d

        @pl.when(k == steps - 1)
        def _():
            out[...] = jnp.exp(acc[...] * SCALE - lt_ref[...]).astype(BF16)

    return pl.pallas_call(
        kernel,
        grid=(steps,),
        in_specs=col_specs([p], chunk) + [whole((1, n))] + col_specs(block, chunk),
        out_specs=whole((ROWS, n)),
        out_shape=jax.ShapeDtypeStruct((ROWS, n), BF16),
        scratch_shapes=[pltpu.VMEM((ROWS, n), F32)],
        compiler_params=params(),
        cost_estimate=cost(2 * ROWS * n * WIDTH, 2 * (ROWS + n) * WIDTH),
        name="back_weights",
    )(p, lt_row, *block)


def body(q, p, hard_owner, hard_row):
    b = lax.axis_index("batch").astype(I32)
    z = (b // 2) % 8
    line_z = (z + jnp.array(OFFSETS, I32)) % 8
    order = z ^ line_z
    line_base = ((b // 16) * 16 + line_z * 2 + b % 2) * ROWS
    group_base = (b ^ jnp.array([0, 1, 16, 17], I32)) * ROWS
    half = ROWS // 2
    xp, xm, zp, zm = _x(1), _x(-1), _z(1), _z(-1)

    ids = (hard_owner * ROWS + hard_row).T
    ids = jnp.concatenate([ids, jnp.full((1, ROWS), -1, I32)], axis=0)

    q_c, ids_c = send(q, SWAP_CORE), send(ids, SWAP_CORE)
    q_c, ids_c, q1, p1 = tie(q_c, ids_c, q, p)
    w, xg, xf = send(p1, SWAP_YL), send(p1, xm), send(p1, xp)
    zg1, zf1 = send(p1, zm), send(p1, zp)
    q1, ids_c, w, xg, xf, zg1, zf1 = tie(q1, ids_c, w, xg, xf, zg1, zf1)

    ids_near = jnp.concatenate([ids, ids_c], axis=1)
    q_y, wg, wf = send(q1, SWAP_YH), send(w, xm), send(w, xp)
    zg2, zf2 = send(zg1, zm), send(zf1, zp)
    ids_far = send(ids_near, SWAP_YH)
    q2, xf, ids_far, q_y, wg, wf, zg2, zf2 = tie(q1, xf, ids_far, q_y, wg, wf, zg2, zf2)

    q_yc, q_l, wg2, xf2 = send(q_y, SWAP_CORE), send(q2, SWAP_YL), send(wg, xm), send(xf, xp)
    zg3, zf3 = send(zg2, zm), send(zf2, zp)
    q_group = [q, q_c, q_y, q_yc]
    ids_group = jnp.concatenate([ids_near, ids_far], axis=1)
    near5 = [p, zf1, zg1, zf2, zg2]
    hs = hard_scores(line_base, (0, 1, 2, 3, 4), ids_group, near5, q_group)
    q3, hs, q_l, wg2, xf2, zg3, zf3 = tie(q2, hs, q_l, wg2, xf2, zg3, zf3)

    qxg, qxf = send(q3, xm), send(q3, xp)
    bottom, top = send(zg3[half:], zm), send(zf3[:half], zp)
    p_block = [p, xf, xg, xf2, w, wf, wg, wg2]
    hs = hs + hard_scores(line_base, (5, 6), ids_group, [zf3, zg3], q_group)
    st = scores(p_block, [q])
    q4, hs, st, bottom, top = tie(q3, hs, st, bottom, top)

    qzg1, qzf1 = send(q4, zm), send(q4, zp)
    hs = hs + hard_scores(line_base, (7,), ids_group, [top, bottom], q_group)
    hs = hs.reshape(8, 2, 2, ROWS)
    mine = hs[:, :, 0] + send(hs[:, :, 1], SWAP_CORE)
    hs = mine[:, 0] + send(mine[:, 1], SWAP_YH)
    hs, qxg, qxf = tie(hs, qxg, qxf)
    lt, loss, w_in, pack = softmax(st, hs, ids)
    other = send(pack[None], _zxor(1))
    pack_near = jnp.concatenate([pack, send(pack, SWAP_CORE)], axis=1)
    pack_far = send(pack_near, SWAP_YH)
    lines = jnp.concatenate([pack[None], other], axis=0)
    pack_near, pack_far, lines, lt, q_l, qxg, qxf, qzg1, qzf1 = tie(
        pack_near, pack_far, lines, lt, q_l, qxg, qxf, qzg1, qzf1
    )

    other = send(lines, _zxor(2))
    other, q_l, qzg1, qzf1, pack_far = tie(other, q_l, qzg1, qzf1, pack_far)
    lines = jnp.concatenate([lines, other], axis=0)
    lt_l = send(lt, SWAP_YL)
    qwg, qwf = send(q_l, xm), send(q_l, xp)
    qzg2, qzf2 = send(qzg1, zm), send(qzf1, zp)
    p_line = [p, zf1, zg1, zf2, zg2, zf3, zg3, top, bottom]
    spec = [SMEM_SPEC, whole((16, 2 * ROWS))]
    h_y, h_yc = hard_grad(fill_forward, [line_base, pack_far], spec, p_line, 2)
    w_in, pack_near, lines, lt_l, h_y, h_yc, qxf, qwg, qwf, qzg2, qzf2 = tie(
        w_in, pack_near, lines, lt_l, h_y, h_yc, qxf, qwg, qwf, qzg2, qzf2
    )

    other = send(lines, _zxor(4))
    other, h_y, h_yc, qxf, qwg, qzg2, qzf2 = tie(other, h_y, h_yc, qxf, qwg, qzg2, qzf2)
    lines = jnp.concatenate([lines, other], axis=0)
    qwg2, qxf2 = send(qwg, xm), send(qxf, xp)
    qzg3, qzf3 = send(qzg2, zm), send(qzf2, zp)
    far_a, far_b, pack_near = tie(*quantize(h_y, send(h_yc, SWAP_CORE)), pack_near)
    far_a = send(far_a, SWAP_YH)
    part, h_c = near_grad(
        fill_forward, [line_base, pack_near], spec, p_line, w_in, p_block, p, 2
    )
    part, h_c, lines, lt, far_a, far_b, qwg2, qxf2, qzg3, qzf3 = tie(
        part, h_c, lines, lt, far_a, far_b, qwg2, qxf2, qzg3, qzf3
    )

    pack4 = send(lines[4], SWAP_CORE)
    q_bottom, q_top = send(qzg3[half:], zm), send(qzf3[:half], zp)
    q_block = [q, qxf, qxg, qxf2, q_l, qwf, qwg, qwg2]
    q_line7 = [q, qzf1, qzg1, qzf2, qzg2, qzf3, qzg3]
    specs = [SMEM_SPEC, SMEM_SPEC, whole((8, 16, ROWS))]

    def fill(first, which):
        return functools.partial(fill_backward, first=first, which=which)

    seven = tuple(range(7))
    h_y, h_yc = hard_grad(fill(2, seven), [group_base, order, lines], specs, q_line7, 2)
    h_yc, lines1 = tie(h_yc, lines)
    h_yc = send(h_yc, SWAP_CORE)
    (h_c2,) = hard_grad(fill(1, seven), [group_base, order, lines1], specs, q_line7, 1)
    h_c, far_b = send(h_c, SWAP_CORE), send(far_b, SWAP_YH)
    pack4, h_y, h_c2, h_c, far_b, q_bottom, q_top = tie(
        pack4, h_y, h_c2, h_c, far_b, q_bottom, q_top
    )

    last = [q_top, q_bottom, send(q_top, SWAP_CORE), send(q_bottom, SWAP_CORE)]
    packs9 = jnp.concatenate([lines, pack4[None]], axis=0)
    order9 = jnp.concatenate([order, jnp.full((1,), 8, I32)])
    specs9 = [SMEM_SPEC, SMEM_SPEC, whole((9, 16, ROWS))]
    small = [group_base, order9, packs9]
    fill_last = functools.partial(fill_backward, first=2, which=(7, 8), groups=1)
    coded = last_far(fill_last, small, specs9, last, (h_y, h_yc))
    lt2 = jnp.concatenate([lt, lt_l], axis=0)
    lt_2, lt_g, lt_f = send(lt2, _x(2)), send(lt2, xm), send(lt2, xp)
    lt_row = jnp.stack([lt2, lt_f, lt_g, lt_2], axis=1).reshape(1, 8 * ROWS)
    h_c2 = send(h_c2, SWAP_CORE)
    coded, far_a, lt_row, h_c2, packs9 = tie(coded, far_a, lt_row, h_c2, packs9)
    far2 = send(coded, SWAP_YH)
    far = jnp.concatenate([dequantize(far_a), dequantize(far_b)], axis=0)
    query_grad = part + h_c + far
    w_back = back_weights(p, q_block, lt_row)
    small = [group_base, order9, packs9]
    (part2,) = near_grad(
        fill(0, tuple(range(9))), small, specs9, q_line7 + last, w_back, q_block, q, 1, (h_c2,)
    )
    passage_grad = part2 + dequantize(far2)
    return loss.reshape(ROWS), query_grad, passage_grad


def solution(mesh):
    rows = P(("blk", "batch"), None)
    return jax.shard_map(
        body,
        mesh=mesh,
        in_specs=(rows, rows, rows, rows),
        out_specs=(P(("blk", "batch")), rows, rows),
        check_vma=False,
    )
```

```python
import functools

import jax
import jax.numpy as jnp
from jax import lax
from jax.experimental import pallas as pl
from jax.experimental.pallas import tpu as pltpu
from jax.sharding import PartitionSpec as P

ROWS = 128
WIDTH = 4096
HARD = 7
SCALE = WIDTH ** (-0.5)
AXES = ("blk", "batch")
VMEM_LIMIT = 12 * 1024 * 1024
F32, BF16, I32, I16 = jnp.float32, jnp.bfloat16, jnp.int32, jnp.int16


def _pairs(move):
    pairs = []
    for i in range(256):
        a, b = divmod(i, 32)
        yl, x = divmod(a, 4)
        yh, rest = divmod(b, 16)
        z, c = divmod(rest, 2)
        yl, x, yh, z, c = move(yl, x, yh, z, c)
        pairs.append((i, (yl * 4 + x) * 32 + yh * 16 + z * 2 + c))
    return pairs


def _x(d):
    return _pairs(lambda yl, x, yh, z, c: (yl, (x + d) % 4, yh, z, c))


def _z(d):
    return _pairs(lambda yl, x, yh, z, c: (yl, x, yh, (z + d) % 8, c))


def _zxor(m):
    return _pairs(lambda yl, x, yh, z, c: (yl, x, yh, z ^ m, c))


SWAP_CORE = _pairs(lambda yl, x, yh, z, c: (yl, x, yh, z, 1 - c))
SWAP_YH = _pairs(lambda yl, x, yh, z, c: (yl, x, 1 - yh, z, c))
SWAP_YL = _pairs(lambda yl, x, yh, z, c: (1 - yl, x, yh, z, c))
OFFSETS = (0, -1, 1, -2, 2, -3, 3, 4)


def send(value, pairs):
    return lax.ppermute(value, AXES, pairs)


def tie(*values):
    return lax.optimization_barrier(values)


def params(**kw):
    return pltpu.CompilerParams(vmem_limit_bytes=VMEM_LIMIT, **kw)


def cost(flops, nbytes):
    return pl.CostEstimate(flops=flops, bytes_accessed=nbytes, transcendentals=0)


def cat(refs):
    return jnp.concatenate([r[...] for r in refs], axis=0)


def nt(l, r):
    return lax.dot_general(l, r, (((1,), (1,)), ((), ())), preferred_element_type=F32)


def whole(shape):
    return pl.BlockSpec(shape, lambda k: tuple(0 for _ in shape))


SMEM_SPEC = pl.BlockSpec(memory_space=pltpu.SMEM)


def col_specs(arrays, chunk):
    return [pl.BlockSpec((a.shape[0], chunk), lambda k: (0, k)) for a in arrays]


def rows_of(arrays):
    return sum(a.shape[0] for a in arrays)


def scores(lhs, rhs, chunk=1024):
    m, n, nl = rows_of(lhs), rows_of(rhs), len(lhs)

    def kernel(*refs):
        out = refs[-1]
        d = nt(cat(refs[:nl]), cat(refs[nl:-1]))
        k = pl.program_id(0)

        @pl.when(k == 0)
        def _():
            out[...] = d

        @pl.when(k > 0)
        def _():
            out[...] += d

    return pl.pallas_call(
        kernel,
        grid=(WIDTH // chunk,),
        in_specs=col_specs(lhs + rhs, chunk),
        out_specs=whole((m, n)),
        out_shape=jax.ShapeDtypeStruct((m, n), F32),
        compiler_params=params(),
        cost_estimate=cost(2 * m * n * WIDTH, 2 * (m + n) * WIDTH + 4 * m * n),
        name="scores",
    )(*lhs, *rhs)


def hard_scores(bases, which, ids, line, group, chunk=1024):
    m, n, nl = rows_of(line), rows_of(group), len(line)
    steps = WIDTH // chunk

    def kernel(base, ids_ref, *refs):
        out, acc = refs[-2], refs[-1]
        d = nt(cat(refs[:nl]), cat(refs[nl:-2]))
        k = pl.program_id(0)

        @pl.when(k == 0)
        def _():
            acc[...] = d

        @pl.when(k > 0)
        def _():
            acc[...] += d

        @pl.when(k == steps - 1)
        def _():
            iota = lax.broadcasted_iota(I32, (ROWS, ROWS), 0)
            for g in range(n // ROWS):
                cols = slice(g * ROWS, (g + 1) * ROWS)
                idg = ids_ref[:, cols]
                sums = [jnp.zeros((1, ROWS), F32) for _ in range(HARD)]
                for i in range(m // ROWS):
                    rel = idg - base[which[i]]
                    s = acc[i * ROWS:(i + 1) * ROWS, cols]
                    for j in range(HARD):
                        hit = jnp.where(iota == rel[j:j + 1], s, 0.0)
                        sums[j] += jnp.sum(hit, axis=0, keepdims=True)
                out[:, cols] = jnp.concatenate(sums + [jnp.zeros((1, ROWS), F32)], axis=0)

    return pl.pallas_call(
        kernel,
        grid=(steps,),
        in_specs=[SMEM_SPEC, whole((8, n))] + col_specs(line + group, chunk),
        out_specs=whole((8, n)),
        out_shape=jax.ShapeDtypeStruct((8, n), F32),
        scratch_shapes=[pltpu.VMEM((m, n), F32)],
        compiler_params=params(),
        cost_estimate=cost(2 * m * n * WIDTH, 2 * (m + n) * WIDTH),
        name="hard_scores",
    )(bases, ids, *line, *group)


def softmax(st, hs, ids):
    m = st.shape[0]

    def kernel(st_ref, hs_ref, ids_ref, lt_ref, loss_ref, w_ref, pack_ref):
        s = st_ref[...] * SCALE
        real = lax.broadcasted_iota(I32, (8, ROWS), 0) < HARD
        h = jnp.where(real, hs_ref[...] * SCALE, -jnp.inf)
        t = jnp.maximum(
            jnp.max(s, axis=0, keepdims=True), jnp.max(h, axis=0, keepdims=True)
        )
        total = jnp.sum(jnp.exp(s - t), axis=0, keepdims=True) + jnp.sum(
            jnp.exp(h - t), axis=0, keepdims=True
        )
        lt = t + jnp.log(total)
        lt_ref[...] = lt
        own = s[:ROWS]
        i0 = lax.broadcasted_iota(I32, (ROWS, ROWS), 0)
        i1 = lax.broadcasted_iota(I32, (ROWS, ROWS), 1)
        loss_ref[...] = lt - jnp.sum(jnp.where(i0 == i1, own, 0.0), axis=0, keepdims=True)
        w = jnp.exp(s - lt)
        for i in range(m // ROWS):
            w_ref[:, i * ROWS:(i + 1) * ROWS] = w[i * ROWS:(i + 1) * ROWS].T.astype(BF16)
        hw = jnp.exp(h - lt).astype(BF16).astype(F32)
        pack_ref[:8] = jnp.where(real, hw, jnp.broadcast_to(lt, (8, ROWS)))
        pack_ref[8:] = ids_ref[...].astype(F32)

    row = jax.ShapeDtypeStruct((1, ROWS), F32)
    return pl.pallas_call(
        kernel,
        out_shape=[
            row,
            row,
            jax.ShapeDtypeStruct((ROWS, m), BF16),
            jax.ShapeDtypeStruct((16, ROWS), F32),
        ],
        compiler_params=params(),
        cost_estimate=cost(10 * m * ROWS, 6 * m * ROWS),
        name="softmax",
    )(st, hs, ids)


def spread_tile(pack, base):
    hw, rel = pack[:8], pack[8:].astype(I32) - base
    iota = lax.broadcasted_iota(I32, (ROWS, ROWS), 0)
    tile = jnp.zeros((ROWS, ROWS), F32)
    for j in range(HARD):
        tile = jnp.where(iota == rel[j:j + 1], hw[j:j + 1], tile)
    return tile


def fill_forward(w, line_base, packs, groups):
    for g in range(groups):
        cols = slice(g * ROWS, (g + 1) * ROWS)
        for i in range(8):
            tile = spread_tile(packs[:, cols], line_base[i])
            w[cols, i * ROWS:(i + 1) * ROWS] = tile.T.astype(BF16)


def fill_backward(w, group_base, order, packs, first, which, groups):
    for i, block in enumerate(which):
        pack = packs[order[block]]
        for g in range(groups):
            tile = spread_tile(pack, group_base[first + g])
            w[g * ROWS:(g + 1) * ROWS, i * ROWS:(i + 1) * ROWS] = tile.astype(BF16)


def hard_grad(fill, small, small_specs, line, groups, chunk=512):
    ns, nl = len(small), len(line)
    depth = rows_of(line)

    def kernel(*refs):
        sm, ln = refs[:ns], refs[ns:ns + nl]
        outs, w = refs[ns + nl:-1], refs[-1]

        @pl.when(pl.program_id(0) == 0)
        def _():
            fill(w, *sm, groups=groups)

        d = jnp.dot(w[...], cat(ln), preferred_element_type=F32)
        for g in range(groups):
            outs[g][...] = d[g * ROWS:(g + 1) * ROWS]

    out = [jax.ShapeDtypeStruct((ROWS, WIDTH), F32)] * groups
    return pl.pallas_call(
        kernel,
        grid=(WIDTH // chunk,),
        in_specs=small_specs + col_specs(line, chunk),
        out_specs=col_specs(out, chunk),
        out_shape=out,
        scratch_shapes=[pltpu.VMEM((groups * ROWS, depth), BF16)],
        compiler_params=params(),
        cost_estimate=cost(
            2 * groups * ROWS * depth * WIDTH, 2 * (depth + 2 * groups * ROWS) * WIDTH
        ),
        name="hard_grad",
    )(*small, *line)


def encode(v, out):
    top = jnp.max(jnp.abs(v), axis=1, keepdims=True)
    e = jnp.ceil(jnp.log2(jnp.maximum(top, 1e-30) / 32000.0))
    out[:, :WIDTH] = jnp.round(v * jnp.exp2(-e)).astype(I32).astype(I16)
    out[:, WIDTH:] = jnp.broadcast_to(e, (v.shape[0], 128)).astype(I32).astype(I16)


def last_far(fill, small, small_specs, line, before, chunk=512):
    ns, nl = len(small), len(line)
    depth = rows_of(line)
    steps = WIDTH // chunk

    def kernel(*refs):
        sm, ln = refs[:ns], refs[ns:ns + nl]
        b0, b1, out, w, total = refs[ns + nl:]
        k = pl.program_id(0)

        @pl.when(k == 0)
        def _():
            fill(w, *sm)

        d = jnp.dot(w[...], cat(ln), preferred_element_type=F32)
        cols = pl.ds(pl.multiple_of(k * chunk, chunk), chunk)
        total[:, cols] = d + b0[...] + b1[...]

        @pl.when(k == steps - 1)
        def _():
            encode(total[...], out)

    return pl.pallas_call(
        kernel,
        grid=(steps,),
        in_specs=small_specs + col_specs(line, chunk) + col_specs(list(before), chunk),
        out_specs=whole((ROWS, WIDTH + 128)),
        out_shape=jax.ShapeDtypeStruct((ROWS, WIDTH + 128), I16),
        scratch_shapes=[pltpu.VMEM((ROWS, depth), BF16), pltpu.VMEM((ROWS, WIDTH), F32)],
        compiler_params=params(),
        cost_estimate=cost(2 * ROWS * depth * WIDTH, 2 * (depth + 5 * ROWS) * WIDTH),
        name="last_far",
    )(*small, *line, *before)


def near_grad(fill, small, small_specs, line, w_in, block, minus, groups, came=(), chunk=512):
    ns, nl, nb, nc = len(small), len(line), len(block), len(came)
    depth = rows_of(line)

    def kernel(*refs):
        sm, ln = refs[:ns], refs[ns:ns + nl]
        w_ref, bl = refs[ns + nl], refs[ns + nl + 1:ns + nl + 1 + nb]
        minus_ref, *rest = refs[ns + nl + 1 + nb:]
        cm, outs, w = rest[:nc], rest[nc:-1], rest[-1]

        @pl.when(pl.program_id(0) == 0)
        def _():
            fill(w, *sm, groups=groups)

        d = jnp.dot(w[...], cat(ln), preferred_element_type=F32)
        e = jnp.dot(w_ref[...], cat(bl), preferred_element_type=F32)
        own = d[:ROWS] + e - minus_ref[...].astype(F32)
        for c in cm:
            own += c[...]
        outs[0][...] = own
        for g in range(1, groups):
            outs[g][...] = d[g * ROWS:(g + 1) * ROWS]

    out = [jax.ShapeDtypeStruct((ROWS, WIDTH), F32)] * groups
    return pl.pallas_call(
        kernel,
        grid=(WIDTH // chunk,),
        in_specs=small_specs
        + col_specs(line, chunk)
        + [whole(w_in.shape)]
        + col_specs(block + [minus] + list(came), chunk),
        out_specs=col_specs(out, chunk),
        out_shape=out,
        scratch_shapes=[pltpu.VMEM((groups * ROWS, depth), BF16)],
        compiler_params=params(),
        cost_estimate=cost(6 * ROWS * 8 * ROWS * WIDTH, 22 * ROWS * 2 * WIDTH),
        name="near_grad",
    )(*small, *line, w_in, *block, minus, *came)


def quantize(a, b):
    half = ROWS // 2

    def kernel(a_ref, b_ref, out0, out1):
        encode(a_ref[:half] + b_ref[:half], out0)
        encode(a_ref[half:] + b_ref[half:], out1)

    out = jax.ShapeDtypeStruct((half, WIDTH + 128), I16)
    return pl.pallas_call(
        kernel,
        out_shape=[out, out],
        compiler_params=params(),
        cost_estimate=cost(6 * ROWS * WIDTH, 10 * ROWS * WIDTH),
        name="quantize",
    )(a, b)


def dequantize(coded):
    step = jnp.exp2(coded[:, WIDTH:WIDTH + 1].astype(F32))
    return coded[:, :WIDTH].astype(F32) * step


def back_weights(p, block, lt_row, chunk=1024):
    nb = len(block)
    n = rows_of(block)
    steps = WIDTH // chunk

    def kernel(p_ref, lt_ref, *refs):
        out, acc = refs[-2], refs[-1]
        d = nt(p_ref[...], cat(refs[:nb]))
        k = pl.program_id(0)

        @pl.when(k == 0)
        def _():
            acc[...] = d

        @pl.when(k > 0)
        def _():
            acc[...] += d

        @pl.when(k == steps - 1)
        def _():
            out[...] = jnp.exp(acc[...] * SCALE - lt_ref[...]).astype(BF16)

    return pl.pallas_call(
        kernel,
        grid=(steps,),
        in_specs=col_specs([p], chunk) + [whole((1, n))] + col_specs(block, chunk),
        out_specs=whole((ROWS, n)),
        out_shape=jax.ShapeDtypeStruct((ROWS, n), BF16),
        scratch_shapes=[pltpu.VMEM((ROWS, n), F32)],
        compiler_params=params(),
        cost_estimate=cost(2 * ROWS * n * WIDTH, 2 * (ROWS + n) * WIDTH),
        name="back_weights",
    )(p, lt_row, *block)


def body(q, p, hard_owner, hard_row):
    b = lax.axis_index("batch").astype(I32)
    z = (b // 2) % 8
    line_z = (z + jnp.array(OFFSETS, I32)) % 8
    order = z ^ line_z
    line_base = ((b // 16) * 16 + line_z * 2 + b % 2) * ROWS
    group_base = (b ^ jnp.array([0, 1, 16, 17], I32)) * ROWS
    half = ROWS // 2
    xp, xm, zp, zm = _x(1), _x(-1), _z(1), _z(-1)

    ids = (hard_owner * ROWS + hard_row).T
    ids = jnp.concatenate([ids, jnp.full((1, ROWS), -1, I32)], axis=0)

    q_c, ids_c = send(q, SWAP_CORE), send(ids, SWAP_CORE)
    ids_near = jnp.concatenate([ids, ids_c], axis=1)
    ids_far = send(ids_near, SWAP_YH)
    q_c, ids_far, q1, p1 = tie(q_c, ids_far, q, p)
    zg1, zf1 = send(p1, zm), send(p1, zp)
    xg, xf, w = send(p1, xm), send(p1, xp), send(p1, SWAP_YL)
    w, q1 = tie(w, q1)
    zg2, zf2 = send(zg1, zm), send(zf1, zp)
    w1, xf1, xg, xf = tie(w, xf, xg, xf)
    wg, wf = send(w1, xm), send(w1, xp)
    q_y = send(q1, SWAP_YH)
    q_y, q2 = tie(q_y, q1)
    wg, wf, xf1 = tie(wg, wf, xf1)
    zg3, zf3 = send(zg2, zm), send(zf2, zp)
    q_yc, q_l, wg2, xf2 = send(q_y, SWAP_CORE), send(q2, SWAP_YL), send(wg, xm), send(xf1, xp)
    q_group = [q, q_c, q_y, q_yc]
    ids_group = jnp.concatenate([ids_near, ids_far], axis=1)
    near5 = [p, zf1, zg1, zf2, zg2]
    hs = hard_scores(line_base, (0, 1, 2, 3, 4), ids_group, near5, q_group)
    q3, hs, q_l, wg2, xf2, zg3, zf3 = tie(q2, hs, q_l, wg2, xf2, zg3, zf3)

    qxg, qxf = send(q3, xm), send(q3, xp)
    bottom, top = send(zg3[half:], zm), send(zf3[:half], zp)
    p_block = [p, xf, xg, xf2, w, wf, wg, wg2]
    hs = hs + hard_scores(line_base, (5, 6), ids_group, [zf3, zg3], q_group)
    st = scores(p_block, [q])
    q4, hs, st, bottom, top = tie(q3, hs, st, bottom, top)

    qzg1, qzf1 = send(q4, zm), send(q4, zp)
    hs = hs + hard_scores(line_base, (7,), ids_group, [top, bottom], q_group)
    hs = hs.reshape(8, 2, 2, ROWS)
    mine = hs[:, :, 0] + send(hs[:, :, 1], SWAP_CORE)
    hs = mine[:, 0] + send(mine[:, 1], SWAP_YH)
    hs, qxg, qxf = tie(hs, qxg, qxf)
    lt, loss, w_in, pack = softmax(st, hs, ids)
    other = send(pack[None], _zxor(1))
    lt2 = jnp.concatenate([lt, send(lt, SWAP_YL)], axis=0)
    pack_near = jnp.concatenate([pack, send(pack, SWAP_CORE)], axis=1)
    pack_far = send(pack_near, SWAP_YH)
    lines = jnp.concatenate([pack[None], other], axis=0)
    pack_near, pack_far, lines, lt2, q_l, qxg, qxf, qzg1, qzf1 = tie(
        pack_near, pack_far, lines, lt2, q_l, qxg, qxf, qzg1, qzf1
    )

    other = send(lines, _zxor(2))
    lt_2, lt_g, lt_f = send(lt2, _x(2)), send(lt2, xm), send(lt2, xp)
    other, lt_2, lt_g, lt_f, q_l, qzg1, qzf1, pack_far = tie(
        other, lt_2, lt_g, lt_f, q_l, qzg1, qzf1, pack_far
    )
    lt_row = jnp.stack([lt2, lt_f, lt_g, lt_2], axis=1).reshape(1, 8 * ROWS)
    lines = jnp.concatenate([lines, other], axis=0)
    qwg, qwf = send(q_l, xm), send(q_l, xp)
    qzg2, qzf2 = send(qzg1, zm), send(qzf1, zp)
    p_line = [p, zf1, zg1, zf2, zg2, zf3, zg3, top, bottom]
    spec = [SMEM_SPEC, whole((16, 2 * ROWS))]
    h_y, h_yc = hard_grad(fill_forward, [line_base, pack_far], spec, p_line, 2)
    w_in, pack_near, lines, h_y, h_yc, qxf, qwg, qwf, qzg2, qzf2 = tie(
        w_in, pack_near, lines, h_y, h_yc, qxf, qwg, qwf, qzg2, qzf2
    )

    other = send(lines, _zxor(4))
    other, qzg2, qzf2 = tie(other, qzg2, qzf2)
    lines = jnp.concatenate([lines, other], axis=0)
    qwg2, qxf2 = send(qwg, xm), send(qxf, xp)
    qzg3, qzf3 = send(qzg2, zm), send(qzf2, zp)
    far_a, far_b, pack_near = tie(*quantize(h_y, send(h_yc, SWAP_CORE)), pack_near)
    far_a = send(far_a, SWAP_YH)
    part, h_c = near_grad(
        fill_forward, [line_base, pack_near], spec, p_line, w_in, p_block, p, 2
    )
    part, h_c, lines, far_a, far_b, qwg2, qxf2, qzg3, qzf3 = tie(
        part, h_c, lines, far_a, far_b, qwg2, qxf2, qzg3, qzf3
    )

    pack4 = send(lines[4], SWAP_CORE)
    q_bottom, q_top = send(qzg3[half:], zm), send(qzf3[:half], zp)
    q_block = [q, qxf, qxg, qxf2, q_l, qwf, qwg, qwg2]
    q_line7 = [q, qzf1, qzg1, qzf2, qzg2, qzf3, qzg3]
    specs = [SMEM_SPEC, SMEM_SPEC, whole((8, 16, ROWS))]

    def fill(first, which):
        return functools.partial(fill_backward, first=first, which=which)

    seven = tuple(range(7))
    h_y, h_yc = hard_grad(fill(2, seven), [group_base, order, lines], specs, q_line7, 2)
    h_yc, lines1 = tie(h_yc, lines)
    h_yc = send(h_yc, SWAP_CORE)
    (h_c2,) = hard_grad(fill(1, seven), [group_base, order, lines1], specs, q_line7, 1)
    h_c, far_b = send(h_c, SWAP_CORE), send(far_b, SWAP_YH)
    pack4, h_y, h_c2, h_c, far_b, q_bottom, q_top = tie(
        pack4, h_y, h_c2, h_c, far_b, q_bottom, q_top
    )

    last = [q_top, q_bottom, send(q_top, SWAP_CORE), send(q_bottom, SWAP_CORE)]
    packs9 = jnp.concatenate([lines, pack4[None]], axis=0)
    order9 = jnp.concatenate([order, jnp.full((1,), 8, I32)])
    specs9 = [SMEM_SPEC, SMEM_SPEC, whole((9, 16, ROWS))]
    small = [group_base, order9, packs9]
    fill_last = functools.partial(fill_backward, first=2, which=(7, 8), groups=1)
    coded = last_far(fill_last, small, specs9, last, (h_y, h_yc))
    h_c2 = send(h_c2, SWAP_CORE)
    coded, far_a, lt_row, h_c2, packs9 = tie(coded, far_a, lt_row, h_c2, packs9)
    far2 = send(coded, SWAP_YH)
    far = jnp.concatenate([dequantize(far_a), dequantize(far_b)], axis=0)
    query_grad = part + h_c + far
    w_back = back_weights(p, q_block, lt_row)
    small = [group_base, order9, packs9]
    (part2,) = near_grad(
        fill(0, tuple(range(9))), small, specs9, q_line7 + last, w_back, q_block, q, 1, (h_c2,)
    )
    passage_grad = part2 + dequantize(far2)
    return loss.reshape(ROWS), query_grad, passage_grad


def solution(mesh):
    rows = P(("blk", "batch"), None)
    return jax.shard_map(
        body,
        mesh=mesh,
        in_specs=(rows, rows, rows, rows),
        out_specs=(P(("blk", "batch")), rows, rows),
        check_vma=False,
    )
```

```python
import functools

import jax
import jax.numpy as jnp
from jax import lax
from jax.experimental import pallas as pl
from jax.experimental.pallas import tpu as pltpu
from jax.sharding import PartitionSpec as P

ROWS = 128
WIDTH = 4096
HARD = 7
SCALE = WIDTH ** (-0.5)
AXES = ("blk", "batch")
VMEM_LIMIT = 12 * 1024 * 1024
F32, BF16, I32, I16 = jnp.float32, jnp.bfloat16, jnp.int32, jnp.int16


def _pairs(move):
    pairs = []
    for i in range(256):
        a, b = divmod(i, 32)
        yl, x = divmod(a, 4)
        yh, rest = divmod(b, 16)
        z, c = divmod(rest, 2)
        yl, x, yh, z, c = move(yl, x, yh, z, c)
        pairs.append((i, (yl * 4 + x) * 32 + yh * 16 + z * 2 + c))
    return pairs


def _x(d):
    return _pairs(lambda yl, x, yh, z, c: (yl, (x + d) % 4, yh, z, c))


def _z(d):
    return _pairs(lambda yl, x, yh, z, c: (yl, x, yh, (z + d) % 8, c))


def _zxor(m):
    return _pairs(lambda yl, x, yh, z, c: (yl, x, yh, z ^ m, c))


SWAP_CORE = _pairs(lambda yl, x, yh, z, c: (yl, x, yh, z, 1 - c))
SWAP_YH = _pairs(lambda yl, x, yh, z, c: (yl, x, 1 - yh, z, c))
SWAP_YL = _pairs(lambda yl, x, yh, z, c: (1 - yl, x, yh, z, c))
OFFSETS = (0, -1, 1, -2, 2, -3, 3, 4)


def send(value, pairs):
    return lax.ppermute(value, AXES, pairs)


def tie(*values):
    return lax.optimization_barrier(values)


def params(**kw):
    return pltpu.CompilerParams(vmem_limit_bytes=VMEM_LIMIT, **kw)


def cost(flops, nbytes):
    return pl.CostEstimate(flops=flops, bytes_accessed=nbytes, transcendentals=0)


def cat(refs):
    return jnp.concatenate([r[...] for r in refs], axis=0)


def nt(l, r):
    return lax.dot_general(l, r, (((1,), (1,)), ((), ())), preferred_element_type=F32)


def whole(shape):
    return pl.BlockSpec(shape, lambda k: tuple(0 for _ in shape))


SMEM_SPEC = pl.BlockSpec(memory_space=pltpu.SMEM)


def col_specs(arrays, chunk):
    return [pl.BlockSpec((a.shape[0], chunk), lambda k: (0, k)) for a in arrays]


def rows_of(arrays):
    return sum(a.shape[0] for a in arrays)


def scores(lhs, rhs, chunk=1024):
    m, n, nl = rows_of(lhs), rows_of(rhs), len(lhs)

    def kernel(*refs):
        out = refs[-1]
        d = nt(cat(refs[:nl]), cat(refs[nl:-1]))
        k = pl.program_id(0)

        @pl.when(k == 0)
        def _():
            out[...] = d

        @pl.when(k > 0)
        def _():
            out[...] += d

    return pl.pallas_call(
        kernel,
        grid=(WIDTH // chunk,),
        in_specs=col_specs(lhs + rhs, chunk),
        out_specs=whole((m, n)),
        out_shape=jax.ShapeDtypeStruct((m, n), F32),
        compiler_params=params(),
        cost_estimate=cost(2 * m * n * WIDTH, 2 * (m + n) * WIDTH + 4 * m * n),
        name="scores",
    )(*lhs, *rhs)


def hard_scores(bases, which, ids, line, group, chunk=1024):
    m, n, nl = rows_of(line), rows_of(group), len(line)
    steps = WIDTH // chunk

    def kernel(base, ids_ref, *refs):
        out, acc = refs[-2], refs[-1]
        d = nt(cat(refs[:nl]), cat(refs[nl:-2]))
        k = pl.program_id(0)

        @pl.when(k == 0)
        def _():
            acc[...] = d

        @pl.when(k > 0)
        def _():
            acc[...] += d

        @pl.when(k == steps - 1)
        def _():
            iota = lax.broadcasted_iota(I32, (ROWS, ROWS), 0)
            for g in range(n // ROWS):
                cols = slice(g * ROWS, (g + 1) * ROWS)
                idg = ids_ref[:, cols]
                sums = [jnp.zeros((1, ROWS), F32) for _ in range(HARD)]
                for i in range(m // ROWS):
                    rel = idg - base[which[i]]
                    s = acc[i * ROWS:(i + 1) * ROWS, cols]
                    for j in range(HARD):
                        hit = jnp.where(iota == rel[j:j + 1], s, 0.0)
                        sums[j] += jnp.sum(hit, axis=0, keepdims=True)
                out[:, cols] = jnp.concatenate(sums + [jnp.zeros((1, ROWS), F32)], axis=0)

    return pl.pallas_call(
        kernel,
        grid=(steps,),
        in_specs=[SMEM_SPEC, whole((8, n))] + col_specs(line + group, chunk),
        out_specs=whole((8, n)),
        out_shape=jax.ShapeDtypeStruct((8, n), F32),
        scratch_shapes=[pltpu.VMEM((m, n), F32)],
        compiler_params=params(),
        cost_estimate=cost(2 * m * n * WIDTH, 2 * (m + n) * WIDTH),
        name="hard_scores",
    )(bases, ids, *line, *group)


def softmax(st, hs, ids):
    m = st.shape[0]

    def kernel(st_ref, hs_ref, ids_ref, lt_ref, loss_ref, w_ref, pack_ref):
        s = st_ref[...] * SCALE
        real = lax.broadcasted_iota(I32, (8, ROWS), 0) < HARD
        h = jnp.where(real, hs_ref[...] * SCALE, -jnp.inf)
        t = jnp.maximum(
            jnp.max(s, axis=0, keepdims=True), jnp.max(h, axis=0, keepdims=True)
        )
        total = jnp.sum(jnp.exp(s - t), axis=0, keepdims=True) + jnp.sum(
            jnp.exp(h - t), axis=0, keepdims=True
        )
        lt = t + jnp.log(total)
        lt_ref[...] = lt
        own = s[:ROWS]
        i0 = lax.broadcasted_iota(I32, (ROWS, ROWS), 0)
        i1 = lax.broadcasted_iota(I32, (ROWS, ROWS), 1)
        loss_ref[...] = lt - jnp.sum(jnp.where(i0 == i1, own, 0.0), axis=0, keepdims=True)
        w = jnp.exp(s - lt)
        for i in range(m // ROWS):
            w_ref[:, i * ROWS:(i + 1) * ROWS] = w[i * ROWS:(i + 1) * ROWS].T.astype(BF16)
        hw = jnp.exp(h - lt).astype(BF16).astype(F32)
        pack_ref[:8] = jnp.where(real, hw, jnp.broadcast_to(lt, (8, ROWS)))
        pack_ref[8:] = ids_ref[...].astype(F32)

    row = jax.ShapeDtypeStruct((1, ROWS), F32)
    return pl.pallas_call(
        kernel,
        out_shape=[
            row,
            row,
            jax.ShapeDtypeStruct((ROWS, m), BF16),
            jax.ShapeDtypeStruct((16, ROWS), F32),
        ],
        compiler_params=params(),
        cost_estimate=cost(10 * m * ROWS, 6 * m * ROWS),
        name="softmax",
    )(st, hs, ids)


def spread_tile(pack, base):
    hw, rel = pack[:8], pack[8:].astype(I32) - base
    iota = lax.broadcasted_iota(I32, (ROWS, ROWS), 0)
    tile = jnp.zeros((ROWS, ROWS), F32)
    for j in range(HARD):
        tile = jnp.where(iota == rel[j:j + 1], hw[j:j + 1], tile)
    return tile


def fill_forward(w, line_base, packs, groups):
    for g in range(groups):
        cols = slice(g * ROWS, (g + 1) * ROWS)
        for i in range(8):
            tile = spread_tile(packs[:, cols], line_base[i])
            w[cols, i * ROWS:(i + 1) * ROWS] = tile.T.astype(BF16)


def fill_backward(w, group_base, order, packs, first, which, groups):
    for i, block in enumerate(which):
        pack = packs[order[block]]
        for g in range(groups):
            tile = spread_tile(pack, group_base[first + g])
            w[g * ROWS:(g + 1) * ROWS, i * ROWS:(i + 1) * ROWS] = tile.astype(BF16)


def hard_grad(fill, small, small_specs, line, groups, chunk=512):
    ns, nl = len(small), len(line)
    depth = rows_of(line)

    def kernel(*refs):
        sm, ln = refs[:ns], refs[ns:ns + nl]
        outs, w = refs[ns + nl:-1], refs[-1]

        @pl.when(pl.program_id(0) == 0)
        def _():
            fill(w, *sm, groups=groups)

        d = jnp.dot(w[...], cat(ln), preferred_element_type=F32)
        for g in range(groups):
            outs[g][...] = d[g * ROWS:(g + 1) * ROWS]

    out = [jax.ShapeDtypeStruct((ROWS, WIDTH), F32)] * groups
    return pl.pallas_call(
        kernel,
        grid=(WIDTH // chunk,),
        in_specs=small_specs + col_specs(line, chunk),
        out_specs=col_specs(out, chunk),
        out_shape=out,
        scratch_shapes=[pltpu.VMEM((groups * ROWS, depth), BF16)],
        compiler_params=params(),
        cost_estimate=cost(
            2 * groups * ROWS * depth * WIDTH, 2 * (depth + 2 * groups * ROWS) * WIDTH
        ),
        name="hard_grad",
    )(*small, *line)


def encode(v, out):
    top = jnp.max(jnp.abs(v), axis=1, keepdims=True)
    e = jnp.ceil(jnp.log2(jnp.maximum(top, 1e-30) / 32000.0))
    out[:, :WIDTH] = jnp.round(v * jnp.exp2(-e)).astype(I32).astype(I16)
    out[:, WIDTH:] = jnp.broadcast_to(e, (v.shape[0], 128)).astype(I32).astype(I16)


def last_far(fill, small, small_specs, line, before, chunk=512):
    ns, nl = len(small), len(line)
    depth = rows_of(line)
    steps = WIDTH // chunk

    def kernel(*refs):
        sm, ln = refs[:ns], refs[ns:ns + nl]
        b0, b1, out, w, total = refs[ns + nl:]
        k = pl.program_id(0)

        @pl.when(k == 0)
        def _():
            fill(w, *sm)

        d = jnp.dot(w[...], cat(ln), preferred_element_type=F32)
        cols = pl.ds(pl.multiple_of(k * chunk, chunk), chunk)
        total[:, cols] = d + b0[...] + b1[...]

        @pl.when(k == steps - 1)
        def _():
            encode(total[...], out)

    return pl.pallas_call(
        kernel,
        grid=(steps,),
        in_specs=small_specs + col_specs(line, chunk) + col_specs(list(before), chunk),
        out_specs=whole((ROWS, WIDTH + 128)),
        out_shape=jax.ShapeDtypeStruct((ROWS, WIDTH + 128), I16),
        scratch_shapes=[pltpu.VMEM((ROWS, depth), BF16), pltpu.VMEM((ROWS, WIDTH), F32)],
        compiler_params=params(),
        cost_estimate=cost(2 * ROWS * depth * WIDTH, 2 * (depth + 5 * ROWS) * WIDTH),
        name="last_far",
    )(*small, *line, *before)


def near_grad(fill, small, small_specs, line, w_in, block, minus, groups, came=(), chunk=512):
    ns, nl, nb, nc = len(small), len(line), len(block), len(came)
    depth = rows_of(line)

    def kernel(*refs):
        sm, ln = refs[:ns], refs[ns:ns + nl]
        w_ref, bl = refs[ns + nl], refs[ns + nl + 1:ns + nl + 1 + nb]
        minus_ref, *rest = refs[ns + nl + 1 + nb:]
        cm, outs, w = rest[:nc], rest[nc:-1], rest[-1]

        @pl.when(pl.program_id(0) == 0)
        def _():
            fill(w, *sm, groups=groups)

        d = jnp.dot(w[...], cat(ln), preferred_element_type=F32)
        e = jnp.dot(w_ref[...], cat(bl), preferred_element_type=F32)
        own = d[:ROWS] + e - minus_ref[...].astype(F32)
        for c in cm:
            own += c[...]
        outs[0][...] = own
        for g in range(1, groups):
            outs[g][...] = d[g * ROWS:(g + 1) * ROWS]

    out = [jax.ShapeDtypeStruct((ROWS, WIDTH), F32)] * groups
    return pl.pallas_call(
        kernel,
        grid=(WIDTH // chunk,),
        in_specs=small_specs
        + col_specs(line, chunk)
        + [whole(w_in.shape)]
        + col_specs(block + [minus] + list(came), chunk),
        out_specs=col_specs(out, chunk),
        out_shape=out,
        scratch_shapes=[pltpu.VMEM((groups * ROWS, depth), BF16)],
        compiler_params=params(),
        cost_estimate=cost(6 * ROWS * 8 * ROWS * WIDTH, 22 * ROWS * 2 * WIDTH),
        name="near_grad",
    )(*small, *line, w_in, *block, minus, *came)


def quantize(a, b):
    half = ROWS // 2

    def kernel(a_ref, b_ref, out0, out1):
        encode(a_ref[:half] + b_ref[:half], out0)
        encode(a_ref[half:] + b_ref[half:], out1)

    out = jax.ShapeDtypeStruct((half, WIDTH + 128), I16)
    return pl.pallas_call(
        kernel,
        out_shape=[out, out],
        compiler_params=params(),
        cost_estimate=cost(6 * ROWS * WIDTH, 10 * ROWS * WIDTH),
        name="quantize",
    )(a, b)


def dequantize(coded):
    step = jnp.exp2(coded[:, WIDTH:WIDTH + 1].astype(F32))
    return coded[:, :WIDTH].astype(F32) * step


def back_weights(p, block, lt_row, chunk=1024):
    nb = len(block)
    n = rows_of(block)
    steps = WIDTH // chunk

    def kernel(p_ref, lt_ref, *refs):
        out, acc = refs[-2], refs[-1]
        d = nt(p_ref[...], cat(refs[:nb]))
        k = pl.program_id(0)

        @pl.when(k == 0)
        def _():
            acc[...] = d

        @pl.when(k > 0)
        def _():
            acc[...] += d

        @pl.when(k == steps - 1)
        def _():
            out[...] = jnp.exp(acc[...] * SCALE - lt_ref[...]).astype(BF16)

    return pl.pallas_call(
        kernel,
        grid=(steps,),
        in_specs=col_specs([p], chunk) + [whole((1, n))] + col_specs(block, chunk),
        out_specs=whole((ROWS, n)),
        out_shape=jax.ShapeDtypeStruct((ROWS, n), BF16),
        scratch_shapes=[pltpu.VMEM((ROWS, n), F32)],
        compiler_params=params(),
        cost_estimate=cost(2 * ROWS * n * WIDTH, 2 * (ROWS + n) * WIDTH),
        name="back_weights",
    )(p, lt_row, *block)


def body(q, p, hard_owner, hard_row):
    b = lax.axis_index("batch").astype(I32)
    z = (b // 2) % 8
    line_z = (z + jnp.array(OFFSETS, I32)) % 8
    order = z ^ line_z
    line_base = ((b // 16) * 16 + line_z * 2 + b % 2) * ROWS
    group_base = (b ^ jnp.array([0, 1, 16, 17], I32)) * ROWS
    half = ROWS // 2
    xp, xm, zp, zm = _x(1), _x(-1), _z(1), _z(-1)

    ids = (hard_owner * ROWS + hard_row).T
    ids = jnp.concatenate([ids, jnp.full((1, ROWS), -1, I32)], axis=0)

    q_c, ids_c = send(q, SWAP_CORE), send(ids, SWAP_CORE)
    ids_near = jnp.concatenate([ids, ids_c], axis=1)
    q_c, ids_near, q1, p1 = tie(q_c, ids_near, q, p)
    zg1, zf1 = send(p1, zm), send(p1, zp)
    ids_far = send(ids_near, SWAP_YH)
    xg, xf, w = send(p1, xm), send(p1, xp), send(p1, SWAP_YL)
    w, q1, ids_far = tie(w, q1, ids_far)
    zg2, zf2 = send(zg1, zm), send(zf1, zp)
    w1, xf1, xg, xf = tie(w, xf, xg, xf)
    wg, wf = send(w1, xm), send(w1, xp)
    q_y = send(q1, SWAP_YH)
    q_y, q2 = tie(q_y, q1)
    wg, wf, xf1 = tie(wg, wf, xf1)
    zg3, zf3 = send(zg2, zm), send(zf2, zp)
    q_yc, q_l, wg2, xf2 = send(q_y, SWAP_CORE), send(q2, SWAP_YL), send(wg, xm), send(xf1, xp)
    q_group = [q, q_c, q_y, q_yc]
    ids_group = jnp.concatenate([ids_near, ids_far], axis=1)
    near5 = [p, zf1, zg1, zf2, zg2]
    hs = hard_scores(line_base, (0, 1, 2, 3, 4), ids_group, near5, q_group)
    q3, hs, q_l, wg2, xf2, zg3, zf3 = tie(q2, hs, q_l, wg2, xf2, zg3, zf3)

    qxg, qxf = send(q3, xm), send(q3, xp)
    bottom, top = send(zg3[half:], zm), send(zf3[:half], zp)
    p_block = [p, xf, xg, xf2, w, wf, wg, wg2]
    hs = hs + hard_scores(line_base, (5, 6), ids_group, [zf3, zg3], q_group)
    st = scores(p_block, [q])
    q4, hs, st, bottom, top = tie(q3, hs, st, bottom, top)

    qzg1, qzf1 = send(q4, zm), send(q4, zp)
    hs = hs + hard_scores(line_base, (7,), ids_group, [top, bottom], q_group)
    hs = hs.reshape(8, 2, 2, ROWS)
    mine = hs[:, :, 0] + send(hs[:, :, 1], SWAP_CORE)
    hs = mine[:, 0] + send(mine[:, 1], SWAP_YH)
    hs, qxg, qxf = tie(hs, qxg, qxf)
    lt, loss, w_in, pack = softmax(st, hs, ids)
    lt2 = jnp.concatenate([lt, send(lt, SWAP_YL)], axis=0)
    pack_near = jnp.concatenate([pack, send(pack, SWAP_CORE)], axis=1)
    pack_far = send(pack_near, SWAP_YH)
    lt_2, lt_g, lt_f = send(lt2, _x(2)), send(lt2, xm), send(lt2, xp)
    lt_row = jnp.stack([lt2, lt_f, lt_g, lt_2], axis=1).reshape(1, 8 * ROWS)
    pack, pack_far, lt_row = tie(pack, pack_far, lt_row)
    other = send(pack[None], _zxor(1))
    lines = jnp.concatenate([pack[None], other], axis=0)
    pack_near, pack_far, lines, lt_row, q_l, qxg, qxf, qzg1, qzf1 = tie(
        pack_near, pack_far, lines, lt_row, q_l, qxg, qxf, qzg1, qzf1
    )

    other = send(lines, _zxor(2))
    lines = jnp.concatenate([lines, other], axis=0)
    qwg, qwf = send(q_l, xm), send(q_l, xp)
    qzg2, qzf2 = send(qzg1, zm), send(qzf1, zp)
    p_line = [p, zf1, zg1, zf2, zg2, zf3, zg3, top, bottom]
    spec = [SMEM_SPEC, whole((16, 2 * ROWS))]
    h_y, h_yc = hard_grad(fill_forward, [line_base, pack_far], spec, p_line, 2)
    w_in, pack_near, lines, h_y, h_yc, qxf, qwg, qwf, qzg2, qzf2 = tie(
        w_in, pack_near, lines, h_y, h_yc, qxf, qwg, qwf, qzg2, qzf2
    )

    other = send(lines, _zxor(4))
    other, qzg2, qzf2 = tie(other, qzg2, qzf2)
    lines = jnp.concatenate([lines, other], axis=0)
    qwg2, qxf2 = send(qwg, xm), send(qxf, xp)
    qzg3, qzf3 = send(qzg2, zm), send(qzf2, zp)
    far_a, far_b, pack_near = tie(*quantize(h_y, send(h_yc, SWAP_CORE)), pack_near)
    far_a = send(far_a, SWAP_YH)
    part, h_c = near_grad(
        fill_forward, [line_base, pack_near], spec, p_line, w_in, p_block, p, 2
    )
    part, h_c, lines, far_a, far_b, qwg2, qxf2, qzg3, qzf3 = tie(
        part, h_c, lines, far_a, far_b, qwg2, qxf2, qzg3, qzf3
    )

    pack4 = send(lines[4], SWAP_CORE)
    q_block = [q, qxf, qxg, qxf2, q_l, qwf, qwg, qwg2]
    q_bottom, q_top = send(qzg3[half:], zm), send(qzf3[:half], zp)
    q_line7 = [q, qzf1, qzg1, qzf2, qzg2, qzf3, qzg3]
    specs = [SMEM_SPEC, SMEM_SPEC, whole((8, 16, ROWS))]

    def fill(first, which):
        return functools.partial(fill_backward, first=first, which=which)

    seven = tuple(range(7))
    h_y, h_yc = hard_grad(fill(2, seven), [group_base, order, lines], specs, q_line7, 2)
    h_yc, lines1, pack4 = tie(h_yc, lines, pack4)
    h_yc = send(h_yc, SWAP_CORE)
    (h_c2,) = hard_grad(fill(1, seven), [group_base, order, lines1], specs, q_line7, 1)
    h_c, far_b = send(h_c, SWAP_CORE), send(far_b, SWAP_YH)
    pack4, h_y, h_c2, h_c, far_b, q_bottom, q_top = tie(
        pack4, h_y, h_c2, h_c, far_b, q_bottom, q_top
    )

    last = [q_top, q_bottom, send(q_top, SWAP_CORE), send(q_bottom, SWAP_CORE)]
    packs9 = jnp.concatenate([lines, pack4[None]], axis=0)
    order9 = jnp.concatenate([order, jnp.full((1,), 8, I32)])
    specs9 = [SMEM_SPEC, SMEM_SPEC, whole((9, 16, ROWS))]
    small = [group_base, order9, packs9]
    fill_last = functools.partial(fill_backward, first=2, which=(7, 8), groups=1)
    coded = last_far(fill_last, small, specs9, last, (h_y, h_yc))
    h_c2 = send(h_c2, SWAP_CORE)
    coded, far_a, lt_row, h_c2, packs9 = tie(coded, far_a, lt_row, h_c2, packs9)
    far2 = send(coded, SWAP_YH)
    far = jnp.concatenate([dequantize(far_a), dequantize(far_b)], axis=0)
    query_grad = part + h_c + far
    w_back = back_weights(p, q_block, lt_row)
    small = [group_base, order9, packs9]
    (part2,) = near_grad(
        fill(0, tuple(range(9))), small, specs9, q_line7 + last, w_back, q_block, q, 1, (h_c2,)
    )
    passage_grad = part2 + dequantize(far2)
    return loss.reshape(ROWS), query_grad, passage_grad


def solution(mesh):
    rows = P(("blk", "batch"), None)
    return jax.shard_map(
        body,
        mesh=mesh,
        in_specs=(rows, rows, rows, rows),
        out_specs=(P(("blk", "batch")), rows, rows),
        check_vma=False,
    )
```

```python
import functools

import jax
import jax.numpy as jnp
from jax import lax
from jax.experimental import pallas as pl
from jax.experimental.pallas import tpu as pltpu
from jax.sharding import PartitionSpec as P

ROWS = 128
WIDTH = 4096
HARD = 7
SCALE = WIDTH ** (-0.5)
AXES = ("blk", "batch")
VMEM_LIMIT = 12 * 1024 * 1024
F32, BF16, I32, I16 = jnp.float32, jnp.bfloat16, jnp.int32, jnp.int16


def _pairs(move):
    pairs = []
    for i in range(256):
        a, b = divmod(i, 32)
        yl, x = divmod(a, 4)
        yh, rest = divmod(b, 16)
        z, c = divmod(rest, 2)
        yl, x, yh, z, c = move(yl, x, yh, z, c)
        pairs.append((i, (yl * 4 + x) * 32 + yh * 16 + z * 2 + c))
    return pairs


def _x(d):
    return _pairs(lambda yl, x, yh, z, c: (yl, (x + d) % 4, yh, z, c))


def _z(d):
    return _pairs(lambda yl, x, yh, z, c: (yl, x, yh, (z + d) % 8, c))


def _zxor(m):
    return _pairs(lambda yl, x, yh, z, c: (yl, x, yh, z ^ m, c))


SWAP_CORE = _pairs(lambda yl, x, yh, z, c: (yl, x, yh, z, 1 - c))
SWAP_YH = _pairs(lambda yl, x, yh, z, c: (yl, x, 1 - yh, z, c))
SWAP_YL = _pairs(lambda yl, x, yh, z, c: (1 - yl, x, yh, z, c))
OFFSETS = (0, -1, 1, -2, 2, -3, 3, 4)


def send(value, pairs):
    return lax.ppermute(value, AXES, pairs)


def tie(*values):
    return lax.optimization_barrier(values)


def params(**kw):
    return pltpu.CompilerParams(vmem_limit_bytes=VMEM_LIMIT, **kw)


def cost(flops, nbytes):
    return pl.CostEstimate(flops=flops, bytes_accessed=nbytes, transcendentals=0)


def cat(refs):
    return jnp.concatenate([r[...] for r in refs], axis=0)


def nt(l, r):
    return lax.dot_general(l, r, (((1,), (1,)), ((), ())), preferred_element_type=F32)


def whole(shape):
    return pl.BlockSpec(shape, lambda k: tuple(0 for _ in shape))


SMEM_SPEC = pl.BlockSpec(memory_space=pltpu.SMEM)


def col_specs(arrays, chunk):
    return [pl.BlockSpec((a.shape[0], chunk), lambda k: (0, k)) for a in arrays]


def rows_of(arrays):
    return sum(a.shape[0] for a in arrays)


def scores(lhs, rhs, chunk=1024):
    m, n, nl = rows_of(lhs), rows_of(rhs), len(lhs)

    def kernel(*refs):
        out = refs[-1]
        d = nt(cat(refs[:nl]), cat(refs[nl:-1]))
        k = pl.program_id(0)

        @pl.when(k == 0)
        def _():
            out[...] = d

        @pl.when(k > 0)
        def _():
            out[...] += d

    return pl.pallas_call(
        kernel,
        grid=(WIDTH // chunk,),
        in_specs=col_specs(lhs + rhs, chunk),
        out_specs=whole((m, n)),
        out_shape=jax.ShapeDtypeStruct((m, n), F32),
        compiler_params=params(),
        cost_estimate=cost(2 * m * n * WIDTH, 2 * (m + n) * WIDTH + 4 * m * n),
        name="scores",
    )(*lhs, *rhs)


def hard_scores(bases, which, ids, line, group, chunk=1024):
    m, n, nl = rows_of(line), rows_of(group), len(line)
    steps = WIDTH // chunk

    def kernel(base, ids_ref, *refs):
        out, acc = refs[-2], refs[-1]
        d = nt(cat(refs[:nl]), cat(refs[nl:-2]))
        k = pl.program_id(0)

        @pl.when(k == 0)
        def _():
            acc[...] = d

        @pl.when(k > 0)
        def _():
            acc[...] += d

        @pl.when(k == steps - 1)
        def _():
            iota = lax.broadcasted_iota(I32, (ROWS, ROWS), 0)
            for g in range(n // ROWS):
                cols = slice(g * ROWS, (g + 1) * ROWS)
                idg = ids_ref[:, cols]
                sums = [jnp.zeros((1, ROWS), F32) for _ in range(HARD)]
                for i in range(m // ROWS):
                    rel = idg - base[which[i]]
                    s = acc[i * ROWS:(i + 1) * ROWS, cols]
                    for j in range(HARD):
                        hit = jnp.where(iota == rel[j:j + 1], s, 0.0)
                        sums[j] += jnp.sum(hit, axis=0, keepdims=True)
                out[:, cols] = jnp.concatenate(sums + [jnp.zeros((1, ROWS), F32)], axis=0)

    return pl.pallas_call(
        kernel,
        grid=(steps,),
        in_specs=[SMEM_SPEC, whole((8, n))] + col_specs(line + group, chunk),
        out_specs=whole((8, n)),
        out_shape=jax.ShapeDtypeStruct((8, n), F32),
        scratch_shapes=[pltpu.VMEM((m, n), F32)],
        compiler_params=params(),
        cost_estimate=cost(2 * m * n * WIDTH, 2 * (m + n) * WIDTH),
        name="hard_scores",
    )(bases, ids, *line, *group)


def softmax(st, hs, ids):
    m = st.shape[0]

    def kernel(st_ref, hs_ref, ids_ref, lt_ref, loss_ref, w_ref, pack_ref):
        s = st_ref[...] * SCALE
        real = lax.broadcasted_iota(I32, (8, ROWS), 0) < HARD
        h = jnp.where(real, hs_ref[...] * SCALE, -jnp.inf)
        t = jnp.maximum(
            jnp.max(s, axis=0, keepdims=True), jnp.max(h, axis=0, keepdims=True)
        )
        total = jnp.sum(jnp.exp(s - t), axis=0, keepdims=True) + jnp.sum(
            jnp.exp(h - t), axis=0, keepdims=True
        )
        lt = t + jnp.log(total)
        lt_ref[...] = lt
        own = s[:ROWS]
        i0 = lax.broadcasted_iota(I32, (ROWS, ROWS), 0)
        i1 = lax.broadcasted_iota(I32, (ROWS, ROWS), 1)
        loss_ref[...] = lt - jnp.sum(jnp.where(i0 == i1, own, 0.0), axis=0, keepdims=True)
        w = jnp.exp(s - lt)
        for i in range(m // ROWS):
            w_ref[:, i * ROWS:(i + 1) * ROWS] = w[i * ROWS:(i + 1) * ROWS].T.astype(BF16)
        hw = jnp.exp(h - lt).astype(BF16).astype(F32)
        pack_ref[:8] = jnp.where(real, hw, jnp.broadcast_to(lt, (8, ROWS)))
        pack_ref[8:] = ids_ref[...].astype(F32)

    row = jax.ShapeDtypeStruct((1, ROWS), F32)
    return pl.pallas_call(
        kernel,
        out_shape=[
            row,
            row,
            jax.ShapeDtypeStruct((ROWS, m), BF16),
            jax.ShapeDtypeStruct((16, ROWS), F32),
        ],
        compiler_params=params(),
        cost_estimate=cost(10 * m * ROWS, 6 * m * ROWS),
        name="softmax",
    )(st, hs, ids)


def spread_tile(pack, base):
    hw, rel = pack[:8], pack[8:].astype(I32) - base
    iota = lax.broadcasted_iota(I32, (ROWS, ROWS), 0)
    tile = jnp.zeros((ROWS, ROWS), F32)
    for j in range(HARD):
        tile = jnp.where(iota == rel[j:j + 1], hw[j:j + 1], tile)
    return tile


def fill_forward(w, line_base, packs, groups):
    for g in range(groups):
        cols = slice(g * ROWS, (g + 1) * ROWS)
        for i in range(8):
            tile = spread_tile(packs[:, cols], line_base[i])
            w[cols, i * ROWS:(i + 1) * ROWS] = tile.T.astype(BF16)


def fill_backward(w, group_base, order, packs, first, which, groups):
    for i, block in enumerate(which):
        pack = packs[order[block]]
        for g in range(groups):
            tile = spread_tile(pack, group_base[first + g])
            w[g * ROWS:(g + 1) * ROWS, i * ROWS:(i + 1) * ROWS] = tile.astype(BF16)


def hard_grad(fill, small, small_specs, line, groups, chunk=512):
    ns, nl = len(small), len(line)
    depth = rows_of(line)

    def kernel(*refs):
        sm, ln = refs[:ns], refs[ns:ns + nl]
        outs, w = refs[ns + nl:-1], refs[-1]

        @pl.when(pl.program_id(0) == 0)
        def _():
            fill(w, *sm, groups=groups)

        d = jnp.dot(w[...], cat(ln), preferred_element_type=F32)
        for g in range(groups):
            outs[g][...] = d[g * ROWS:(g + 1) * ROWS]

    out = [jax.ShapeDtypeStruct((ROWS, WIDTH), F32)] * groups
    return pl.pallas_call(
        kernel,
        grid=(WIDTH // chunk,),
        in_specs=small_specs + col_specs(line, chunk),
        out_specs=col_specs(out, chunk),
        out_shape=out,
        scratch_shapes=[pltpu.VMEM((groups * ROWS, depth), BF16)],
        compiler_params=params(),
        cost_estimate=cost(
            2 * groups * ROWS * depth * WIDTH, 2 * (depth + 2 * groups * ROWS) * WIDTH
        ),
        name="hard_grad",
    )(*small, *line)


def encode(v, out):
    top = jnp.max(jnp.abs(v), axis=1, keepdims=True)
    e = jnp.ceil(jnp.log2(jnp.maximum(top, 1e-30) / 32000.0))
    out[:, :WIDTH] = jnp.round(v * jnp.exp2(-e)).astype(I32).astype(I16)
    out[:, WIDTH:] = jnp.broadcast_to(e, (v.shape[0], 128)).astype(I32).astype(I16)


def last_far(fill, small, small_specs, line, before, chunk=512):
    ns, nl = len(small), len(line)
    depth = rows_of(line)
    steps = WIDTH // chunk

    def kernel(*refs):
        sm, ln = refs[:ns], refs[ns:ns + nl]
        b0, b1, out, w, total = refs[ns + nl:]
        k = pl.program_id(0)

        @pl.when(k == 0)
        def _():
            fill(w, *sm)

        d = jnp.dot(w[...], cat(ln), preferred_element_type=F32)
        cols = pl.ds(pl.multiple_of(k * chunk, chunk), chunk)
        total[:, cols] = d + b0[...] + b1[...]

        @pl.when(k == steps - 1)
        def _():
            encode(total[...], out)

    return pl.pallas_call(
        kernel,
        grid=(steps,),
        in_specs=small_specs + col_specs(line, chunk) + col_specs(list(before), chunk),
        out_specs=whole((ROWS, WIDTH + 128)),
        out_shape=jax.ShapeDtypeStruct((ROWS, WIDTH + 128), I16),
        scratch_shapes=[pltpu.VMEM((ROWS, depth), BF16), pltpu.VMEM((ROWS, WIDTH), F32)],
        compiler_params=params(),
        cost_estimate=cost(2 * ROWS * depth * WIDTH, 2 * (depth + 5 * ROWS) * WIDTH),
        name="last_far",
    )(*small, *line, *before)


def near_grad(fill, small, small_specs, line, w_in, block, minus, groups, came=(), chunk=512):
    ns, nl, nb, nc = len(small), len(line), len(block), len(came)
    depth = rows_of(line)

    def kernel(*refs):
        sm, ln = refs[:ns], refs[ns:ns + nl]
        w_ref, bl = refs[ns + nl], refs[ns + nl + 1:ns + nl + 1 + nb]
        minus_ref, *rest = refs[ns + nl + 1 + nb:]
        cm, outs, w = rest[:nc], rest[nc:-1], rest[-1]

        @pl.when(pl.program_id(0) == 0)
        def _():
            fill(w, *sm, groups=groups)

        d = jnp.dot(w[...], cat(ln), preferred_element_type=F32)
        e = jnp.dot(w_ref[...], cat(bl), preferred_element_type=F32)
        own = d[:ROWS] + e - minus_ref[...].astype(F32)
        for c in cm:
            own += c[...]
        outs[0][...] = own
        for g in range(1, groups):
            outs[g][...] = d[g * ROWS:(g + 1) * ROWS]

    out = [jax.ShapeDtypeStruct((ROWS, WIDTH), F32)] * groups
    return pl.pallas_call(
        kernel,
        grid=(WIDTH // chunk,),
        in_specs=small_specs
        + col_specs(line, chunk)
        + [whole(w_in.shape)]
        + col_specs(block + [minus] + list(came), chunk),
        out_specs=col_specs(out, chunk),
        out_shape=out,
        scratch_shapes=[pltpu.VMEM((groups * ROWS, depth), BF16)],
        compiler_params=params(),
        cost_estimate=cost(6 * ROWS * 8 * ROWS * WIDTH, 22 * ROWS * 2 * WIDTH),
        name="near_grad",
    )(*small, *line, w_in, *block, minus, *came)


def quantize(a, b):
    half = ROWS // 2

    def kernel(a_ref, b_ref, out0, out1):
        encode(a_ref[:half] + b_ref[:half], out0)
        encode(a_ref[half:] + b_ref[half:], out1)

    out = jax.ShapeDtypeStruct((half, WIDTH + 128), I16)
    return pl.pallas_call(
        kernel,
        out_shape=[out, out],
        compiler_params=params(),
        cost_estimate=cost(6 * ROWS * WIDTH, 10 * ROWS * WIDTH),
        name="quantize",
    )(a, b)


def dequantize(coded):
    step = jnp.exp2(coded[:, WIDTH:WIDTH + 1].astype(F32))
    return coded[:, :WIDTH].astype(F32) * step


def back_weights(p, block, lt_row, chunk=1024):
    nb = len(block)
    n = rows_of(block)
    steps = WIDTH // chunk

    def kernel(p_ref, lt_ref, *refs):
        out, acc = refs[-2], refs[-1]
        d = nt(p_ref[...], cat(refs[:nb]))
        k = pl.program_id(0)

        @pl.when(k == 0)
        def _():
            acc[...] = d

        @pl.when(k > 0)
        def _():
            acc[...] += d

        @pl.when(k == steps - 1)
        def _():
            out[...] = jnp.exp(acc[...] * SCALE - lt_ref[...]).astype(BF16)

    return pl.pallas_call(
        kernel,
        grid=(steps,),
        in_specs=col_specs([p], chunk) + [whole((1, n))] + col_specs(block, chunk),
        out_specs=whole((ROWS, n)),
        out_shape=jax.ShapeDtypeStruct((ROWS, n), BF16),
        scratch_shapes=[pltpu.VMEM((ROWS, n), F32)],
        compiler_params=params(),
        cost_estimate=cost(2 * ROWS * n * WIDTH, 2 * (ROWS + n) * WIDTH),
        name="back_weights",
    )(p, lt_row, *block)


def body(q, p, hard_owner, hard_row):
    b = lax.axis_index("batch").astype(I32)
    z = (b // 2) % 8
    line_z = (z + jnp.array(OFFSETS, I32)) % 8
    order = z ^ line_z
    line_base = ((b // 16) * 16 + line_z * 2 + b % 2) * ROWS
    group_base = (b ^ jnp.array([0, 1, 16, 17], I32)) * ROWS
    half = ROWS // 2
    xp, xm, zp, zm = _x(1), _x(-1), _z(1), _z(-1)

    ids = (hard_owner * ROWS + hard_row).T
    ids = jnp.concatenate([ids, jnp.full((1, ROWS), -1, I32)], axis=0)

    q_c, ids_c = send(q, SWAP_CORE), send(ids, SWAP_CORE)
    ids_near = jnp.concatenate([ids, ids_c], axis=1)
    q_c, ids_near, q1, p1 = tie(q_c, ids_near, q, p)
    zg1, zf1 = send(p1, zm), send(p1, zp)
    ids_far = send(ids_near, SWAP_YH)
    ids_far, p2 = tie(ids_far, p1)
    xg, xf, w = send(p1, xm), send(p1, xp), send(p2, SWAP_YL)
    w, q1 = tie(w, q1)
    zg2, zf2 = send(zg1, zm), send(zf1, zp)
    w1, xf1, xg, xf = tie(w, xf, xg, xf)
    wg, wf = send(w1, xm), send(w1, xp)
    q_y = send(q1, SWAP_YH)
    q_y, q2 = tie(q_y, q1)
    wg, wf, xf1 = tie(wg, wf, xf1)
    zg3, zf3 = send(zg2, zm), send(zf2, zp)
    q_yc, q_l, wg2, xf2 = send(q_y, SWAP_CORE), send(q2, SWAP_YL), send(wg, xm), send(xf1, xp)
    q_group = [q, q_c, q_y, q_yc]
    ids_group = jnp.concatenate([ids_near, ids_far], axis=1)
    near5 = [p, zf1, zg1, zf2, zg2]
    hs = hard_scores(line_base, (0, 1, 2, 3, 4), ids_group, near5, q_group)
    q3, hs, q_l, wg2, xf2, zg3, zf3 = tie(q2, hs, q_l, wg2, xf2, zg3, zf3)

    qxg, qxf = send(q3, xm), send(q3, xp)
    bottom, top = send(zg3[half:], zm), send(zf3[:half], zp)
    p_block = [p, xf, xg, xf2, w, wf, wg, wg2]
    hs = hs + hard_scores(line_base, (5, 6), ids_group, [zf3, zg3], q_group)
    st = scores(p_block, [q])
    q4, hs, st, bottom, top = tie(q3, hs, st, bottom, top)

    qzg1, qzf1 = send(q4, zm), send(q4, zp)
    hs = hs + hard_scores(line_base, (7,), ids_group, [top, bottom], q_group)
    hs = hs.reshape(8, 2, 2, ROWS)
    mine = hs[:, :, 0] + send(hs[:, :, 1], SWAP_CORE)
    hs = mine[:, 0] + send(mine[:, 1], SWAP_YH)
    hs, qxg, qxf = tie(hs, qxg, qxf)
    lt, loss, w_in, pack = softmax(st, hs, ids)
    lt2 = jnp.concatenate([lt, send(lt, SWAP_YL)], axis=0)
    pack_near = jnp.concatenate([pack, send(pack, SWAP_CORE)], axis=1)
    pack_far = send(pack_near, SWAP_YH)
    lt_2, lt_g, lt_f = send(lt2, _x(2)), send(lt2, xm), send(lt2, xp)
    lt_row = jnp.stack([lt2, lt_f, lt_g, lt_2], axis=1).reshape(1, 8 * ROWS)
    pack, pack_far, lt_row = tie(pack, pack_far, lt_row)
    other = send(pack[None], _zxor(1))
    lines = jnp.concatenate([pack[None], other], axis=0)
    pack_near, pack_far, lines, lt_row, q_l, qxg, qxf, qzg1, qzf1 = tie(
        pack_near, pack_far, lines, lt_row, q_l, qxg, qxf, qzg1, qzf1
    )

    other = send(lines, _zxor(2))
    lines = jnp.concatenate([lines, other], axis=0)
    qwg, qwf = send(q_l, xm), send(q_l, xp)
    qzg2, qzf2 = send(qzg1, zm), send(qzf1, zp)
    p_line = [p, zf1, zg1, zf2, zg2, zf3, zg3, top, bottom]
    spec = [SMEM_SPEC, whole((16, 2 * ROWS))]
    h_y, h_yc = hard_grad(fill_forward, [line_base, pack_far], spec, p_line, 2)
    w_in, pack_near, lines, h_y, h_yc, qxf, qwg, qwf, qzg2, qzf2 = tie(
        w_in, pack_near, lines, h_y, h_yc, qxf, qwg, qwf, qzg2, qzf2
    )

    other = send(lines, _zxor(4))
    other, qzg2, qzf2 = tie(other, qzg2, qzf2)
    lines = jnp.concatenate([lines, other], axis=0)
    qwg2, qxf2 = send(qwg, xm), send(qxf, xp)
    qzg3, qzf3 = send(qzg2, zm), send(qzf2, zp)
    far_a, far_b, pack_near = tie(*quantize(h_y, send(h_yc, SWAP_CORE)), pack_near)
    far_a = send(far_a, SWAP_YH)
    part, h_c = near_grad(
        fill_forward, [line_base, pack_near], spec, p_line, w_in, p_block, p, 2
    )
    part, h_c, lines, far_a, far_b, qwg2, qxf2, qzg3, qzf3 = tie(
        part, h_c, lines, far_a, far_b, qwg2, qxf2, qzg3, qzf3
    )

    pack4 = send(lines[4], SWAP_CORE)
    q_block = [q, qxf, qxg, qxf2, q_l, qwf, qwg, qwg2]
    q_bottom, q_top = send(qzg3[half:], zm), send(qzf3[:half], zp)
    q_line7 = [q, qzf1, qzg1, qzf2, qzg2, qzf3, qzg3]
    specs = [SMEM_SPEC, SMEM_SPEC, whole((8, 16, ROWS))]

    def fill(first, which):
        return functools.partial(fill_backward, first=first, which=which)

    seven = tuple(range(7))
    h_y, h_yc = hard_grad(fill(2, seven), [group_base, order, lines], specs, q_line7, 2)
    h_yc, lines1, pack4 = tie(h_yc, lines, pack4)
    h_yc = send(h_yc, SWAP_CORE)
    (h_c2,) = hard_grad(fill(1, seven), [group_base, order, lines1], specs, q_line7, 1)
    h_c, far_b = send(h_c, SWAP_CORE), send(far_b, SWAP_YH)
    pack4, h_y, h_c2, h_c, far_b, q_bottom, q_top = tie(
        pack4, h_y, h_c2, h_c, far_b, q_bottom, q_top
    )

    last = [q_top, q_bottom, send(q_top, SWAP_CORE), send(q_bottom, SWAP_CORE)]
    packs9 = jnp.concatenate([lines, pack4[None]], axis=0)
    order9 = jnp.concatenate([order, jnp.full((1,), 8, I32)])
    specs9 = [SMEM_SPEC, SMEM_SPEC, whole((9, 16, ROWS))]
    small = [group_base, order9, packs9]
    fill_last = functools.partial(fill_backward, first=2, which=(7, 8), groups=1)
    coded = last_far(fill_last, small, specs9, last, (h_y, h_yc))
    h_c2 = send(h_c2, SWAP_CORE)
    coded, far_a, lt_row, h_c2, packs9 = tie(coded, far_a, lt_row, h_c2, packs9)
    far2 = send(coded, SWAP_YH)
    far = jnp.concatenate([dequantize(far_a), dequantize(far_b)], axis=0)
    query_grad = part + h_c + far
    w_back = back_weights(p, q_block, lt_row)
    small = [group_base, order9, packs9]
    (part2,) = near_grad(
        fill(0, tuple(range(9))), small, specs9, q_line7 + last, w_back, q_block, q, 1, (h_c2,)
    )
    passage_grad = part2 + dequantize(far2)
    return loss.reshape(ROWS), query_grad, passage_grad


def solution(mesh):
    rows = P(("blk", "batch"), None)
    return jax.shard_map(
        body,
        mesh=mesh,
        in_specs=(rows, rows, rows, rows),
        out_specs=(P(("blk", "batch")), rows, rows),
        check_vma=False,
    )
```

```python
import functools

import jax
import jax.numpy as jnp
from jax import lax
from jax.experimental import pallas as pl
from jax.experimental.pallas import tpu as pltpu
from jax.sharding import PartitionSpec as P

ROWS = 128
WIDTH = 4096
HARD = 7
SCALE = WIDTH ** (-0.5)
AXES = ("blk", "batch")
VMEM_LIMIT = 12 * 1024 * 1024
F32, BF16, I32, I16 = jnp.float32, jnp.bfloat16, jnp.int32, jnp.int16


def _pairs(move):
    pairs = []
    for i in range(256):
        a, b = divmod(i, 32)
        yl, x = divmod(a, 4)
        yh, rest = divmod(b, 16)
        z, c = divmod(rest, 2)
        yl, x, yh, z, c = move(yl, x, yh, z, c)
        pairs.append((i, (yl * 4 + x) * 32 + yh * 16 + z * 2 + c))
    return pairs


def _x(d):
    return _pairs(lambda yl, x, yh, z, c: (yl, (x + d) % 4, yh, z, c))


def _z(d):
    return _pairs(lambda yl, x, yh, z, c: (yl, x, yh, (z + d) % 8, c))


def _zxor(m):
    return _pairs(lambda yl, x, yh, z, c: (yl, x, yh, z ^ m, c))


SWAP_CORE = _pairs(lambda yl, x, yh, z, c: (yl, x, yh, z, 1 - c))
SWAP_YH = _pairs(lambda yl, x, yh, z, c: (yl, x, 1 - yh, z, c))
SWAP_YL = _pairs(lambda yl, x, yh, z, c: (1 - yl, x, yh, z, c))
OFFSETS = (0, -1, 1, -2, 2, -3, 3, 4)


def send(value, pairs):
    return lax.ppermute(value, AXES, pairs)


def tie(*values):
    return lax.optimization_barrier(values)


def params(**kw):
    return pltpu.CompilerParams(vmem_limit_bytes=VMEM_LIMIT, **kw)


def cost(flops, nbytes):
    return pl.CostEstimate(flops=flops, bytes_accessed=nbytes, transcendentals=0)


def cat(refs):
    return jnp.concatenate([r[...] for r in refs], axis=0)


def nt(l, r):
    return lax.dot_general(l, r, (((1,), (1,)), ((), ())), preferred_element_type=F32)


def whole(shape):
    return pl.BlockSpec(shape, lambda k: tuple(0 for _ in shape))


SMEM_SPEC = pl.BlockSpec(memory_space=pltpu.SMEM)


def col_specs(arrays, chunk):
    return [pl.BlockSpec((a.shape[0], chunk), lambda k: (0, k)) for a in arrays]


def rows_of(arrays):
    return sum(a.shape[0] for a in arrays)


def scores(lhs, rhs, chunk=1024):
    m, n, nl = rows_of(lhs), rows_of(rhs), len(lhs)

    def kernel(*refs):
        out = refs[-1]
        d = nt(cat(refs[:nl]), cat(refs[nl:-1]))
        k = pl.program_id(0)

        @pl.when(k == 0)
        def _():
            out[...] = d

        @pl.when(k > 0)
        def _():
            out[...] += d

    return pl.pallas_call(
        kernel,
        grid=(WIDTH // chunk,),
        in_specs=col_specs(lhs + rhs, chunk),
        out_specs=whole((m, n)),
        out_shape=jax.ShapeDtypeStruct((m, n), F32),
        compiler_params=params(),
        cost_estimate=cost(2 * m * n * WIDTH, 2 * (m + n) * WIDTH + 4 * m * n),
        name="scores",
    )(*lhs, *rhs)


def hard_scores(bases, which, ids, line, group, chunk=1024):
    m, n, nl = rows_of(line), rows_of(group), len(line)
    steps = WIDTH // chunk

    def kernel(base, ids_ref, *refs):
        out, acc = refs[-2], refs[-1]
        d = nt(cat(refs[:nl]), cat(refs[nl:-2]))
        k = pl.program_id(0)

        @pl.when(k == 0)
        def _():
            acc[...] = d

        @pl.when(k > 0)
        def _():
            acc[...] += d

        @pl.when(k == steps - 1)
        def _():
            iota = lax.broadcasted_iota(I32, (ROWS, ROWS), 0)
            for g in range(n // ROWS):
                cols = slice(g * ROWS, (g + 1) * ROWS)
                idg = ids_ref[:, cols]
                sums = [jnp.zeros((1, ROWS), F32) for _ in range(HARD)]
                for i in range(m // ROWS):
                    rel = idg - base[which[i]]
                    s = acc[i * ROWS:(i + 1) * ROWS, cols]
                    for j in range(HARD):
                        hit = jnp.where(iota == rel[j:j + 1], s, 0.0)
                        sums[j] += jnp.sum(hit, axis=0, keepdims=True)
                out[:, cols] = jnp.concatenate(sums + [jnp.zeros((1, ROWS), F32)], axis=0)

    return pl.pallas_call(
        kernel,
        grid=(steps,),
        in_specs=[SMEM_SPEC, whole((8, n))] + col_specs(line + group, chunk),
        out_specs=whole((8, n)),
        out_shape=jax.ShapeDtypeStruct((8, n), F32),
        scratch_shapes=[pltpu.VMEM((m, n), F32)],
        compiler_params=params(),
        cost_estimate=cost(2 * m * n * WIDTH, 2 * (m + n) * WIDTH),
        name="hard_scores",
    )(bases, ids, *line, *group)


def softmax(st, hs, ids):
    m = st.shape[0]

    def kernel(st_ref, hs_ref, ids_ref, lt_ref, loss_ref, w_ref, pack_ref):
        s = st_ref[...] * SCALE
        real = lax.broadcasted_iota(I32, (8, ROWS), 0) < HARD
        h = jnp.where(real, hs_ref[...] * SCALE, -jnp.inf)
        t = jnp.maximum(
            jnp.max(s, axis=0, keepdims=True), jnp.max(h, axis=0, keepdims=True)
        )
        total = jnp.sum(jnp.exp(s - t), axis=0, keepdims=True) + jnp.sum(
            jnp.exp(h - t), axis=0, keepdims=True
        )
        lt = t + jnp.log(total)
        lt_ref[...] = lt
        own = s[:ROWS]
        i0 = lax.broadcasted_iota(I32, (ROWS, ROWS), 0)
        i1 = lax.broadcasted_iota(I32, (ROWS, ROWS), 1)
        loss_ref[...] = lt - jnp.sum(jnp.where(i0 == i1, own, 0.0), axis=0, keepdims=True)
        w = jnp.exp(s - lt)
        for i in range(m // ROWS):
            w_ref[:, i * ROWS:(i + 1) * ROWS] = w[i * ROWS:(i + 1) * ROWS].T.astype(BF16)
        hw = jnp.exp(h - lt).astype(BF16).astype(F32)
        pack_ref[:8] = jnp.where(real, hw, jnp.broadcast_to(lt, (8, ROWS)))
        pack_ref[8:] = ids_ref[...].astype(F32)

    row = jax.ShapeDtypeStruct((1, ROWS), F32)
    return pl.pallas_call(
        kernel,
        out_shape=[
            row,
            row,
            jax.ShapeDtypeStruct((ROWS, m), BF16),
            jax.ShapeDtypeStruct((16, ROWS), F32),
        ],
        compiler_params=params(),
        cost_estimate=cost(10 * m * ROWS, 6 * m * ROWS),
        name="softmax",
    )(st, hs, ids)


def spread_tile(pack, base):
    hw, rel = pack[:8], pack[8:].astype(I32) - base
    iota = lax.broadcasted_iota(I32, (ROWS, ROWS), 0)
    tile = jnp.zeros((ROWS, ROWS), F32)
    for j in range(HARD):
        tile = jnp.where(iota == rel[j:j + 1], hw[j:j + 1], tile)
    return tile


def fill_forward(w, line_base, packs, groups):
    for g in range(groups):
        cols = slice(g * ROWS, (g + 1) * ROWS)
        for i in range(8):
            tile = spread_tile(packs[:, cols], line_base[i])
            w[cols, i * ROWS:(i + 1) * ROWS] = tile.T.astype(BF16)


def fill_backward(w, group_base, order, packs, first, which, groups):
    for i, block in enumerate(which):
        pack = packs[order[block]]
        for g in range(groups):
            tile = spread_tile(pack, group_base[first + g])
            w[g * ROWS:(g + 1) * ROWS, i * ROWS:(i + 1) * ROWS] = tile.astype(BF16)


def hard_grad(fill, small, small_specs, line, groups, chunk=512):
    ns, nl = len(small), len(line)
    depth = rows_of(line)

    def kernel(*refs):
        sm, ln = refs[:ns], refs[ns:ns + nl]
        outs, w = refs[ns + nl:-1], refs[-1]

        @pl.when(pl.program_id(0) == 0)
        def _():
            fill(w, *sm, groups=groups)

        d = jnp.dot(w[...], cat(ln), preferred_element_type=F32)
        for g in range(groups):
            outs[g][...] = d[g * ROWS:(g + 1) * ROWS]

    out = [jax.ShapeDtypeStruct((ROWS, WIDTH), F32)] * groups
    return pl.pallas_call(
        kernel,
        grid=(WIDTH // chunk,),
        in_specs=small_specs + col_specs(line, chunk),
        out_specs=col_specs(out, chunk),
        out_shape=out,
        scratch_shapes=[pltpu.VMEM((groups * ROWS, depth), BF16)],
        compiler_params=params(),
        cost_estimate=cost(
            2 * groups * ROWS * depth * WIDTH, 2 * (depth + 2 * groups * ROWS) * WIDTH
        ),
        name="hard_grad",
    )(*small, *line)


def encode(v, out):
    top = jnp.max(jnp.abs(v), axis=1, keepdims=True)
    e = jnp.ceil(jnp.log2(jnp.maximum(top, 1e-30) / 32000.0))
    out[:, :WIDTH] = jnp.round(v * jnp.exp2(-e)).astype(I32).astype(I16)
    out[:, WIDTH:] = jnp.broadcast_to(e, (v.shape[0], 128)).astype(I32).astype(I16)


def last_far(fill, small, small_specs, line, before, chunk=512):
    ns, nl = len(small), len(line)
    depth = rows_of(line)
    steps = WIDTH // chunk

    def kernel(*refs):
        sm, ln = refs[:ns], refs[ns:ns + nl]
        b0, b1, out, w, total = refs[ns + nl:]
        k = pl.program_id(0)

        @pl.when(k == 0)
        def _():
            fill(w, *sm)

        d = jnp.dot(w[...], cat(ln), preferred_element_type=F32)
        cols = pl.ds(pl.multiple_of(k * chunk, chunk), chunk)
        total[:, cols] = d + b0[...] + b1[...]

        @pl.when(k == steps - 1)
        def _():
            encode(total[...], out)

    return pl.pallas_call(
        kernel,
        grid=(steps,),
        in_specs=small_specs + col_specs(line, chunk) + col_specs(list(before), chunk),
        out_specs=whole((ROWS, WIDTH + 128)),
        out_shape=jax.ShapeDtypeStruct((ROWS, WIDTH + 128), I16),
        scratch_shapes=[pltpu.VMEM((ROWS, depth), BF16), pltpu.VMEM((ROWS, WIDTH), F32)],
        compiler_params=params(),
        cost_estimate=cost(2 * ROWS * depth * WIDTH, 2 * (depth + 5 * ROWS) * WIDTH),
        name="last_far",
    )(*small, *line, *before)


def near_grad(fill, small, small_specs, line, w_in, block, minus, groups, came=(), chunk=512):
    ns, nl, nb, nc = len(small), len(line), len(block), len(came)
    depth = rows_of(line)

    def kernel(*refs):
        sm, ln = refs[:ns], refs[ns:ns + nl]
        w_ref, bl = refs[ns + nl], refs[ns + nl + 1:ns + nl + 1 + nb]
        minus_ref, *rest = refs[ns + nl + 1 + nb:]
        cm, outs, w = rest[:nc], rest[nc:-1], rest[-1]

        @pl.when(pl.program_id(0) == 0)
        def _():
            fill(w, *sm, groups=groups)

        d = jnp.dot(w[...], cat(ln), preferred_element_type=F32)
        e = jnp.dot(w_ref[...], cat(bl), preferred_element_type=F32)
        own = d[:ROWS] + e - minus_ref[...].astype(F32)
        for c in cm:
            own += c[...]
        outs[0][...] = own
        for g in range(1, groups):
            outs[g][...] = d[g * ROWS:(g + 1) * ROWS]

    out = [jax.ShapeDtypeStruct((ROWS, WIDTH), F32)] * groups
    return pl.pallas_call(
        kernel,
        grid=(WIDTH // chunk,),
        in_specs=small_specs
        + col_specs(line, chunk)
        + [whole(w_in.shape)]
        + col_specs(block + [minus] + list(came), chunk),
        out_specs=col_specs(out, chunk),
        out_shape=out,
        scratch_shapes=[pltpu.VMEM((groups * ROWS, depth), BF16)],
        compiler_params=params(),
        cost_estimate=cost(6 * ROWS * 8 * ROWS * WIDTH, 22 * ROWS * 2 * WIDTH),
        name="near_grad",
    )(*small, *line, w_in, *block, minus, *came)


def quantize(a, b):
    half = ROWS // 2

    def kernel(a_ref, b_ref, out0, out1):
        encode(a_ref[:half] + b_ref[:half], out0)
        encode(a_ref[half:] + b_ref[half:], out1)

    out = jax.ShapeDtypeStruct((half, WIDTH + 128), I16)
    return pl.pallas_call(
        kernel,
        out_shape=[out, out],
        compiler_params=params(),
        cost_estimate=cost(6 * ROWS * WIDTH, 10 * ROWS * WIDTH),
        name="quantize",
    )(a, b)


def dequantize(coded):
    step = jnp.exp2(coded[:, WIDTH:WIDTH + 1].astype(F32))
    return coded[:, :WIDTH].astype(F32) * step


def back_weights(p, block, lt_row, chunk=1024):
    nb = len(block)
    n = rows_of(block)
    steps = WIDTH // chunk

    def kernel(p_ref, lt_ref, *refs):
        out, acc = refs[-2], refs[-1]
        d = nt(p_ref[...], cat(refs[:nb]))
        k = pl.program_id(0)

        @pl.when(k == 0)
        def _():
            acc[...] = d

        @pl.when(k > 0)
        def _():
            acc[...] += d

        @pl.when(k == steps - 1)
        def _():
            out[...] = jnp.exp(acc[...] * SCALE - lt_ref[...]).astype(BF16)

    return pl.pallas_call(
        kernel,
        grid=(steps,),
        in_specs=col_specs([p], chunk) + [whole((1, n))] + col_specs(block, chunk),
        out_specs=whole((ROWS, n)),
        out_shape=jax.ShapeDtypeStruct((ROWS, n), BF16),
        scratch_shapes=[pltpu.VMEM((ROWS, n), F32)],
        compiler_params=params(),
        cost_estimate=cost(2 * ROWS * n * WIDTH, 2 * (ROWS + n) * WIDTH),
        name="back_weights",
    )(p, lt_row, *block)


def body(q, p, hard_owner, hard_row):
    b = lax.axis_index("batch").astype(I32)
    z = (b // 2) % 8
    line_z = (z + jnp.array(OFFSETS, I32)) % 8
    step = z ^ line_z
    order = (step // 4) + (step & 2) + (step & 1) * 4
    line_base = ((b // 16) * 16 + line_z * 2 + b % 2) * ROWS
    group_base = (b ^ jnp.array([0, 1, 16, 17], I32)) * ROWS
    half = ROWS // 2
    xp, xm, zp, zm = _x(1), _x(-1), _z(1), _z(-1)

    ids = (hard_owner * ROWS + hard_row).T
    ids = jnp.concatenate([ids, jnp.full((1, ROWS), -1, I32)], axis=0)

    q_c, ids_c = send(q, SWAP_CORE), send(ids, SWAP_CORE)
    zg1, zf1 = send(p, zm), send(p, zp)
    xg, xf, w = send(p, xm), send(p, xp), send(p, SWAP_YL)
    w, q_c, ids_c, q1 = tie(w, q_c, ids_c, q)
    zg2, zf2 = send(zg1, zm), send(zf1, zp)
    w1, xf1, xg, xf = tie(w, xf, xg, xf)
    wg, wf = send(w1, xm), send(w1, xp)
    q_y = send(q1, SWAP_YH)
    ids_near = jnp.concatenate([ids, ids_c], axis=1)
    q_y, ids_near, q1 = tie(q_y, ids_near, q1)
    ids_far = send(ids_near, SWAP_YH)
    ids_far, q2 = tie(ids_far, q1)
    wg, wf, xf1 = tie(wg, wf, xf1)
    zg3, zf3 = send(zg2, zm), send(zf2, zp)
    q_yc, q_l, wg2, xf2 = send(q_y, SWAP_CORE), send(q2, SWAP_YL), send(wg, xm), send(xf1, xp)
    q_group = [q, q_c, q_y, q_yc]
    ids_group = jnp.concatenate([ids_near, ids_far], axis=1)
    near5 = [p, zf1, zg1, zf2, zg2]
    hs = hard_scores(line_base, (0, 1, 2, 3, 4), ids_group, near5, q_group)
    q3, hs, wg2, xf2, zg3, zf3 = tie(q2, hs, wg2, xf2, zg3, zf3)

    qxg, qxf = send(q3, xm), send(q3, xp)
    bottom, top = send(zg3[half:], zm), send(zf3[:half], zp)
    p_block = [p, xf, xg, xf2, w, wf, wg, wg2]
    hs = hs + hard_scores(line_base, (5, 6), ids_group, [zf3, zg3], q_group)
    st = scores(p_block, [q])
    q4, hs, st, q_l, bottom, top = tie(q3, hs, st, q_l, bottom, top)

    qzg1, qzf1 = send(q4, zm), send(q4, zp)
    hs = hs + hard_scores(line_base, (7,), ids_group, [top, bottom], q_group)
    hs = hs.reshape(8, 2, 2, ROWS)
    mine = hs[:, :, 0] + send(hs[:, :, 1], SWAP_CORE)
    hs = mine[:, 0] + send(mine[:, 1], SWAP_YH)
    hs, qxg, qxf = tie(hs, qxg, qxf)
    lt, loss, w_in, pack = softmax(st, hs, ids)
    lt2 = jnp.concatenate([lt, send(lt, SWAP_YL)], axis=0)
    pack_near = jnp.concatenate([pack, send(pack, SWAP_CORE)], axis=1)
    pack_far = send(pack_near, SWAP_YH)
    lt_2, lt_g, lt_f = send(lt2, _x(2)), send(lt2, xm), send(lt2, xp)
    lt_row = jnp.stack([lt2, lt_f, lt_g, lt_2], axis=1).reshape(1, 8 * ROWS)
    pack, pack_far, lt_row = tie(pack, pack_far, lt_row)
    other = send(pack[None], _zxor(4))
    lines = jnp.concatenate([pack[None], other], axis=0)
    pack_near, pack_far, lines, lt_row, q_l, qxg, qxf, qzg1, qzf1 = tie(
        pack_near, pack_far, lines, lt_row, q_l, qxg, qxf, qzg1, qzf1
    )

    other = send(lines, _zxor(2))
    lines = jnp.concatenate([lines, other], axis=0)
    qwg, qwf = send(q_l, xm), send(q_l, xp)
    qzg2, qzf2 = send(qzg1, zm), send(qzf1, zp)
    p_line = [p, zf1, zg1, zf2, zg2, zf3, zg3, top, bottom]
    spec = [SMEM_SPEC, whole((16, 2 * ROWS))]
    h_y, h_yc = hard_grad(fill_forward, [line_base, pack_far], spec, p_line, 2)
    w_in, pack_near, lines, h_y, h_yc, qxf, qwg, qwf, qzg2, qzf2 = tie(
        w_in, pack_near, lines, h_y, h_yc, qxf, qwg, qwf, qzg2, qzf2
    )

    other = send(lines, _zxor(1))
    other, qzg2, qzf2 = tie(other, qzg2, qzf2)
    lines = jnp.concatenate([lines, other], axis=0)
    qwg2, qxf2 = send(qwg, xm), send(qxf, xp)
    qzg3, qzf3 = send(qzg2, zm), send(qzf2, zp)
    far_a, far_b, pack_near = tie(*quantize(h_y, send(h_yc, SWAP_CORE)), pack_near)
    far_a = send(far_a, SWAP_YH)
    part, h_c = near_grad(
        fill_forward, [line_base, pack_near], spec, p_line, w_in, p_block, p, 2
    )
    part, h_c, lines, far_a, far_b, qwg2, qxf2, qzg3, qzf3 = tie(
        part, h_c, lines, far_a, far_b, qwg2, qxf2, qzg3, qzf3
    )

    pack4 = send(lines[1], SWAP_CORE)
    q_block = [q, qxf, qxg, qxf2, q_l, qwf, qwg, qwg2]
    q_bottom, q_top = send(qzg3[half:], zm), send(qzf3[:half], zp)
    q_line7 = [q, qzf1, qzg1, qzf2, qzg2, qzf3, qzg3]
    specs = [SMEM_SPEC, SMEM_SPEC, whole((8, 16, ROWS))]

    def fill(first, which):
        return functools.partial(fill_backward, first=first, which=which)

    seven = tuple(range(7))
    h_y, h_yc = hard_grad(fill(2, seven), [group_base, order, lines], specs, q_line7, 2)
    h_yc, lines1, pack4 = tie(h_yc, lines, pack4)
    h_yc = send(h_yc, SWAP_CORE)
    (h_c2,) = hard_grad(fill(1, seven), [group_base, order, lines1], specs, q_line7, 1)
    h_c, far_b = send(h_c, SWAP_CORE), send(far_b, SWAP_YH)
    pack4, h_y, h_c2, h_c, far_b, q_bottom, q_top = tie(
        pack4, h_y, h_c2, h_c, far_b, q_bottom, q_top
    )

    last = [q_top, q_bottom, send(q_top, SWAP_CORE), send(q_bottom, SWAP_CORE)]
    packs9 = jnp.concatenate([lines, pack4[None]], axis=0)
    order9 = jnp.concatenate([order, jnp.full((1,), 8, I32)])
    specs9 = [SMEM_SPEC, SMEM_SPEC, whole((9, 16, ROWS))]
    small = [group_base, order9, packs9]
    fill_last = functools.partial(fill_backward, first=2, which=(7, 8), groups=1)
    coded = last_far(fill_last, small, specs9, last, (h_y, h_yc))
    h_c2 = send(h_c2, SWAP_CORE)
    coded, far_a, lt_row, h_c2, packs9 = tie(coded, far_a, lt_row, h_c2, packs9)
    far2 = send(coded, SWAP_YH)
    far = jnp.concatenate([dequantize(far_a), dequantize(far_b)], axis=0)
    query_grad = part + h_c + far
    w_back = back_weights(p, q_block, lt_row)
    small = [group_base, order9, packs9]
    (part2,) = near_grad(
        fill(0, tuple(range(9))), small, specs9, q_line7 + last, w_back, q_block, q, 1, (h_c2,)
    )
    passage_grad = part2 + dequantize(far2)
    return loss.reshape(ROWS), query_grad, passage_grad


def solution(mesh):
    rows = P(("blk", "batch"), None)
    return jax.shard_map(
        body,
        mesh=mesh,
        in_specs=(rows, rows, rows, rows),
        out_specs=(P(("blk", "batch")), rows, rows),
        check_vma=False,
    )
```

```python
import functools

import jax
import jax.numpy as jnp
from jax import lax
from jax.experimental import pallas as pl
from jax.experimental.pallas import tpu as pltpu
from jax.sharding import PartitionSpec as P

ROWS = 128
WIDTH = 4096
HARD = 7
SCALE = WIDTH ** (-0.5)
AXES = ("blk", "batch")
VMEM_LIMIT = 12 * 1024 * 1024
F32, BF16, I32, I16 = jnp.float32, jnp.bfloat16, jnp.int32, jnp.int16


def _pairs(move):
    pairs = []
    for i in range(256):
        a, b = divmod(i, 32)
        yl, x = divmod(a, 4)
        yh, rest = divmod(b, 16)
        z, c = divmod(rest, 2)
        yl, x, yh, z, c = move(yl, x, yh, z, c)
        pairs.append((i, (yl * 4 + x) * 32 + yh * 16 + z * 2 + c))
    return pairs


def _x(d):
    return _pairs(lambda yl, x, yh, z, c: (yl, (x + d) % 4, yh, z, c))


def _z(d):
    return _pairs(lambda yl, x, yh, z, c: (yl, x, yh, (z + d) % 8, c))


def _zxor(m):
    return _pairs(lambda yl, x, yh, z, c: (yl, x, yh, z ^ m, c))


SWAP_CORE = _pairs(lambda yl, x, yh, z, c: (yl, x, yh, z, 1 - c))
SWAP_YH = _pairs(lambda yl, x, yh, z, c: (yl, x, 1 - yh, z, c))
SWAP_YL = _pairs(lambda yl, x, yh, z, c: (1 - yl, x, yh, z, c))
OFFSETS = (0, -1, 1, -2, 2, -3, 3, 4)


def send(value, pairs):
    return lax.ppermute(value, AXES, pairs)


def tie(*values):
    return lax.optimization_barrier(values)


def params(**kw):
    return pltpu.CompilerParams(vmem_limit_bytes=VMEM_LIMIT, **kw)


def cost(flops, nbytes):
    return pl.CostEstimate(flops=flops, bytes_accessed=nbytes, transcendentals=0)


def cat(refs):
    return jnp.concatenate([r[...] for r in refs], axis=0)


def nt(l, r):
    return lax.dot_general(l, r, (((1,), (1,)), ((), ())), preferred_element_type=F32)


def whole(shape):
    return pl.BlockSpec(shape, lambda k: tuple(0 for _ in shape))


SMEM_SPEC = pl.BlockSpec(memory_space=pltpu.SMEM)


def col_specs(arrays, chunk):
    return [pl.BlockSpec((a.shape[0], chunk), lambda k: (0, k)) for a in arrays]


def rows_of(arrays):
    return sum(a.shape[0] for a in arrays)


def scores(lhs, rhs, chunk=1024):
    m, n, nl = rows_of(lhs), rows_of(rhs), len(lhs)

    def kernel(*refs):
        out = refs[-1]
        d = nt(cat(refs[:nl]), cat(refs[nl:-1]))
        k = pl.program_id(0)

        @pl.when(k == 0)
        def _():
            out[...] = d

        @pl.when(k > 0)
        def _():
            out[...] += d

    return pl.pallas_call(
        kernel,
        grid=(WIDTH // chunk,),
        in_specs=col_specs(lhs + rhs, chunk),
        out_specs=whole((m, n)),
        out_shape=jax.ShapeDtypeStruct((m, n), F32),
        compiler_params=params(),
        cost_estimate=cost(2 * m * n * WIDTH, 2 * (m + n) * WIDTH + 4 * m * n),
        name="scores",
    )(*lhs, *rhs)


def hard_scores(bases, which, ids, line, group, chunk=1024):
    m, n, nl = rows_of(line), rows_of(group), len(line)
    steps = WIDTH // chunk

    def kernel(base, ids_ref, *refs):
        out, acc = refs[-2], refs[-1]
        d = nt(cat(refs[:nl]), cat(refs[nl:-2]))
        k = pl.program_id(0)

        @pl.when(k == 0)
        def _():
            acc[...] = d

        @pl.when(k > 0)
        def _():
            acc[...] += d

        @pl.when(k == steps - 1)
        def _():
            iota = lax.broadcasted_iota(I32, (ROWS, ROWS), 0)
            for g in range(n // ROWS):
                cols = slice(g * ROWS, (g + 1) * ROWS)
                idg = ids_ref[:, cols]
                sums = [jnp.zeros((1, ROWS), F32) for _ in range(HARD)]
                for i in range(m // ROWS):
                    rel = idg - base[which[i]]
                    s = acc[i * ROWS:(i + 1) * ROWS, cols]
                    for j in range(HARD):
                        hit = jnp.where(iota == rel[j:j + 1], s, 0.0)
                        sums[j] += jnp.sum(hit, axis=0, keepdims=True)
                out[:, cols] = jnp.concatenate(sums + [jnp.zeros((1, ROWS), F32)], axis=0)

    return pl.pallas_call(
        kernel,
        grid=(steps,),
        in_specs=[SMEM_SPEC, whole((8, n))] + col_specs(line + group, chunk),
        out_specs=whole((8, n)),
        out_shape=jax.ShapeDtypeStruct((8, n), F32),
        scratch_shapes=[pltpu.VMEM((m, n), F32)],
        compiler_params=params(),
        cost_estimate=cost(2 * m * n * WIDTH, 2 * (m + n) * WIDTH),
        name="hard_scores",
    )(bases, ids, *line, *group)


def softmax(st, hs, ids):
    m = st.shape[0]

    def kernel(st_ref, hs_ref, ids_ref, lt_ref, loss_ref, w_ref, pack_ref):
        s = st_ref[...] * SCALE
        real = lax.broadcasted_iota(I32, (8, ROWS), 0) < HARD
        h = jnp.where(real, hs_ref[...] * SCALE, -jnp.inf)
        t = jnp.maximum(
            jnp.max(s, axis=0, keepdims=True), jnp.max(h, axis=0, keepdims=True)
        )
        total = jnp.sum(jnp.exp(s - t), axis=0, keepdims=True) + jnp.sum(
            jnp.exp(h - t), axis=0, keepdims=True
        )
        lt = t + jnp.log(total)
        lt_ref[...] = lt
        own = s[:ROWS]
        i0 = lax.broadcasted_iota(I32, (ROWS, ROWS), 0)
        i1 = lax.broadcasted_iota(I32, (ROWS, ROWS), 1)
        loss_ref[...] = lt - jnp.sum(jnp.where(i0 == i1, own, 0.0), axis=0, keepdims=True)
        w = jnp.exp(s - lt)
        for i in range(m // ROWS):
            w_ref[:, i * ROWS:(i + 1) * ROWS] = w[i * ROWS:(i + 1) * ROWS].T.astype(BF16)
        hw = jnp.exp(h - lt).astype(BF16).astype(F32)
        pack_ref[:8] = jnp.where(real, hw, jnp.broadcast_to(lt, (8, ROWS)))
        pack_ref[8:] = ids_ref[...].astype(F32)

    row = jax.ShapeDtypeStruct((1, ROWS), F32)
    return pl.pallas_call(
        kernel,
        out_shape=[
            row,
            row,
            jax.ShapeDtypeStruct((ROWS, m), BF16),
            jax.ShapeDtypeStruct((16, ROWS), F32),
        ],
        compiler_params=params(),
        cost_estimate=cost(10 * m * ROWS, 6 * m * ROWS),
        name="softmax",
    )(st, hs, ids)


def spread_tile(pack, base):
    hw, rel = pack[:8], pack[8:].astype(I32) - base
    iota = lax.broadcasted_iota(I32, (ROWS, ROWS), 0)
    tile = jnp.zeros((ROWS, ROWS), F32)
    for j in range(HARD):
        tile = jnp.where(iota == rel[j:j + 1], hw[j:j + 1], tile)
    return tile


def fill_forward(w, line_base, packs, groups):
    for g in range(groups):
        cols = slice(g * ROWS, (g + 1) * ROWS)
        for i in range(8):
            tile = spread_tile(packs[:, cols], line_base[i])
            w[cols, i * ROWS:(i + 1) * ROWS] = tile.T.astype(BF16)


def fill_backward(w, group_base, order, packs, first, which, groups):
    for i, block in enumerate(which):
        pack = packs[order[block]]
        for g in range(groups):
            tile = spread_tile(pack, group_base[first + g])
            w[g * ROWS:(g + 1) * ROWS, i * ROWS:(i + 1) * ROWS] = tile.astype(BF16)


def hard_grad(fill, small, small_specs, line, groups, chunk=512):
    ns, nl = len(small), len(line)
    depth = rows_of(line)

    def kernel(*refs):
        sm, ln = refs[:ns], refs[ns:ns + nl]
        outs, w = refs[ns + nl:-1], refs[-1]

        @pl.when(pl.program_id(0) == 0)
        def _():
            fill(w, *sm, groups=groups)

        d = jnp.dot(w[...], cat(ln), preferred_element_type=F32)
        for g in range(groups):
            outs[g][...] = d[g * ROWS:(g + 1) * ROWS]

    out = [jax.ShapeDtypeStruct((ROWS, WIDTH), F32)] * groups
    return pl.pallas_call(
        kernel,
        grid=(WIDTH // chunk,),
        in_specs=small_specs + col_specs(line, chunk),
        out_specs=col_specs(out, chunk),
        out_shape=out,
        scratch_shapes=[pltpu.VMEM((groups * ROWS, depth), BF16)],
        compiler_params=params(),
        cost_estimate=cost(
            2 * groups * ROWS * depth * WIDTH, 2 * (depth + 2 * groups * ROWS) * WIDTH
        ),
        name="hard_grad",
    )(*small, *line)


def encode(v, out):
    top = jnp.max(jnp.abs(v), axis=1, keepdims=True)
    e = jnp.ceil(jnp.log2(jnp.maximum(top, 1e-30) / 32000.0))
    out[:, :WIDTH] = jnp.round(v * jnp.exp2(-e)).astype(I32).astype(I16)
    out[:, WIDTH:] = jnp.broadcast_to(e, (v.shape[0], 128)).astype(I32).astype(I16)


def last_far(fill, small, small_specs, line, before, chunk=512):
    ns, nl = len(small), len(line)
    depth = rows_of(line)
    steps = WIDTH // chunk

    def kernel(*refs):
        sm, ln = refs[:ns], refs[ns:ns + nl]
        b0, b1, out, w, total = refs[ns + nl:]
        k = pl.program_id(0)

        @pl.when(k == 0)
        def _():
            fill(w, *sm)

        d = jnp.dot(w[...], cat(ln), preferred_element_type=F32)
        cols = pl.ds(pl.multiple_of(k * chunk, chunk), chunk)
        total[:, cols] = d + b0[...] + b1[...]

        @pl.when(k == steps - 1)
        def _():
            encode(total[...], out)

    return pl.pallas_call(
        kernel,
        grid=(steps,),
        in_specs=small_specs + col_specs(line, chunk) + col_specs(list(before), chunk),
        out_specs=whole((ROWS, WIDTH + 128)),
        out_shape=jax.ShapeDtypeStruct((ROWS, WIDTH + 128), I16),
        scratch_shapes=[pltpu.VMEM((ROWS, depth), BF16), pltpu.VMEM((ROWS, WIDTH), F32)],
        compiler_params=params(),
        cost_estimate=cost(2 * ROWS * depth * WIDTH, 2 * (depth + 5 * ROWS) * WIDTH),
        name="last_far",
    )(*small, *line, *before)


def near_grad(fill, small, small_specs, line, w_in, block, minus, groups, came=(), chunk=512):
    ns, nl, nb, nc = len(small), len(line), len(block), len(came)
    depth = rows_of(line)

    def kernel(*refs):
        sm, ln = refs[:ns], refs[ns:ns + nl]
        w_ref, bl = refs[ns + nl], refs[ns + nl + 1:ns + nl + 1 + nb]
        minus_ref, *rest = refs[ns + nl + 1 + nb:]
        cm, outs, w = rest[:nc], rest[nc:-1], rest[-1]

        @pl.when(pl.program_id(0) == 0)
        def _():
            fill(w, *sm, groups=groups)

        d = jnp.dot(w[...], cat(ln), preferred_element_type=F32)
        e = jnp.dot(w_ref[...], cat(bl), preferred_element_type=F32)
        own = d[:ROWS] + e - minus_ref[...].astype(F32)
        for c in cm:
            own += c[...]
        outs[0][...] = own
        for g in range(1, groups):
            outs[g][...] = d[g * ROWS:(g + 1) * ROWS]

    out = [jax.ShapeDtypeStruct((ROWS, WIDTH), F32)] * groups
    return pl.pallas_call(
        kernel,
        grid=(WIDTH // chunk,),
        in_specs=small_specs
        + col_specs(line, chunk)
        + [whole(w_in.shape)]
        + col_specs(block + [minus] + list(came), chunk),
        out_specs=col_specs(out, chunk),
        out_shape=out,
        scratch_shapes=[pltpu.VMEM((groups * ROWS, depth), BF16)],
        compiler_params=params(),
        cost_estimate=cost(6 * ROWS * 8 * ROWS * WIDTH, 22 * ROWS * 2 * WIDTH),
        name="near_grad",
    )(*small, *line, w_in, *block, minus, *came)


def quantize(a, b):
    half = ROWS // 2

    def kernel(a_ref, b_ref, out0, out1):
        encode(a_ref[:half] + b_ref[:half], out0)
        encode(a_ref[half:] + b_ref[half:], out1)

    out = jax.ShapeDtypeStruct((half, WIDTH + 128), I16)
    return pl.pallas_call(
        kernel,
        out_shape=[out, out],
        compiler_params=params(),
        cost_estimate=cost(6 * ROWS * WIDTH, 10 * ROWS * WIDTH),
        name="quantize",
    )(a, b)


def dequantize(coded):
    step = jnp.exp2(coded[:, WIDTH:WIDTH + 1].astype(F32))
    return coded[:, :WIDTH].astype(F32) * step


def back_weights(p, block, lt_row, chunk=1024):
    nb = len(block)
    n = rows_of(block)
    steps = WIDTH // chunk

    def kernel(p_ref, lt_ref, *refs):
        out, acc = refs[-2], refs[-1]
        d = nt(p_ref[...], cat(refs[:nb]))
        k = pl.program_id(0)

        @pl.when(k == 0)
        def _():
            acc[...] = d

        @pl.when(k > 0)
        def _():
            acc[...] += d

        @pl.when(k == steps - 1)
        def _():
            out[...] = jnp.exp(acc[...] * SCALE - lt_ref[...]).astype(BF16)

    return pl.pallas_call(
        kernel,
        grid=(steps,),
        in_specs=col_specs([p], chunk) + [whole((1, n))] + col_specs(block, chunk),
        out_specs=whole((ROWS, n)),
        out_shape=jax.ShapeDtypeStruct((ROWS, n), BF16),
        scratch_shapes=[pltpu.VMEM((ROWS, n), F32)],
        compiler_params=params(),
        cost_estimate=cost(2 * ROWS * n * WIDTH, 2 * (ROWS + n) * WIDTH),
        name="back_weights",
    )(p, lt_row, *block)


def body(q, p, hard_owner, hard_row):
    b = lax.axis_index("batch").astype(I32)
    z = (b // 2) % 8
    line_z = (z + jnp.array(OFFSETS, I32)) % 8
    step = z ^ line_z
    order = (step // 4) + (step & 2) + (step & 1) * 4
    line_base = ((b // 16) * 16 + line_z * 2 + b % 2) * ROWS
    group_base = (b ^ jnp.array([0, 1, 16, 17], I32)) * ROWS
    half = ROWS // 2
    xp, xm, zp, zm = _x(1), _x(-1), _z(1), _z(-1)

    ids = (hard_owner * ROWS + hard_row).T
    ids = jnp.concatenate([ids, jnp.full((1, ROWS), -1, I32)], axis=0)

    q_c, ids_c = send(q, SWAP_CORE), send(ids, SWAP_CORE)
    q_c, ids_c, p1 = tie(q_c, ids_c, p)
    zg1, zf1 = send(p1, zm), send(p1, zp)
    xg, xf, w = send(p, xm), send(p, xp), send(p, SWAP_YL)
    w, q_c, ids_c, q1 = tie(w, q_c, ids_c, q)
    zg2, zf2 = send(zg1, zm), send(zf1, zp)
    w1, xf1, xg, xf = tie(w, xf, xg, xf)
    wg, wf = send(w1, xm), send(w1, xp)
    q_y = send(q1, SWAP_YH)
    ids_near = jnp.concatenate([ids, ids_c], axis=1)
    q_y, ids_near, q1 = tie(q_y, ids_near, q1)
    ids_far = send(ids_near, SWAP_YH)
    ids_far, q2 = tie(ids_far, q1)
    wg, wf, xf1 = tie(wg, wf, xf1)
    zg3, zf3 = send(zg2, zm), send(zf2, zp)
    q_yc, q_l, wg2, xf2 = send(q_y, SWAP_CORE), send(q2, SWAP_YL), send(wg, xm), send(xf1, xp)
    q_group = [q, q_c, q_y, q_yc]
    ids_group = jnp.concatenate([ids_near, ids_far], axis=1)
    near5 = [p, zf1, zg1, zf2, zg2]
    hs = hard_scores(line_base, (0, 1, 2, 3, 4), ids_group, near5, q_group)
    q3, hs, wg2, xf2, zg3, zf3 = tie(q2, hs, wg2, xf2, zg3, zf3)

    qxg, qxf = send(q3, xm), send(q3, xp)
    bottom, top = send(zg3[half:], zm), send(zf3[:half], zp)
    p_block = [p, xf, xg, xf2, w, wf, wg, wg2]
    hs = hs + hard_scores(line_base, (5, 6), ids_group, [zf3, zg3], q_group)
    st = scores(p_block, [q])
    q4, hs, st, q_l, bottom, top = tie(q3, hs, st, q_l, bottom, top)

    qzg1, qzf1 = send(q4, zm), send(q4, zp)
    hs = hs + hard_scores(line_base, (7,), ids_group, [top, bottom], q_group)
    hs = hs.reshape(8, 2, 2, ROWS)
    mine = hs[:, :, 0] + send(hs[:, :, 1], SWAP_CORE)
    hs = mine[:, 0] + send(mine[:, 1], SWAP_YH)
    hs, qxg, qxf = tie(hs, qxg, qxf)
    lt, loss, w_in, pack = softmax(st, hs, ids)
    lt2 = jnp.concatenate([lt, send(lt, SWAP_YL)], axis=0)
    pack_near = jnp.concatenate([pack, send(pack, SWAP_CORE)], axis=1)
    pack_far = send(pack_near, SWAP_YH)
    lt_2, lt_g, lt_f = send(lt2, _x(2)), send(lt2, xm), send(lt2, xp)
    lt_row = jnp.stack([lt2, lt_f, lt_g, lt_2], axis=1).reshape(1, 8 * ROWS)
    pack, pack_far, lt_row = tie(pack, pack_far, lt_row)
    other = send(pack[None], _zxor(4))
    lines = jnp.concatenate([pack[None], other], axis=0)
    pack_near, pack_far, lines, lt_row, q_l, qxg, qxf, qzg1, qzf1 = tie(
        pack_near, pack_far, lines, lt_row, q_l, qxg, qxf, qzg1, qzf1
    )

    other = send(lines, _zxor(2))
    lines = jnp.concatenate([lines, other], axis=0)
    qwg, qwf = send(q_l, xm), send(q_l, xp)
    qzg2, qzf2 = send(qzg1, zm), send(qzf1, zp)
    p_line = [p, zf1, zg1, zf2, zg2, zf3, zg3, top, bottom]
    spec = [SMEM_SPEC, whole((16, 2 * ROWS))]
    h_y, h_yc = hard_grad(fill_forward, [line_base, pack_far], spec, p_line, 2)
    w_in, pack_near, lines, h_y, h_yc, qxf, qwg, qwf, qzg2, qzf2 = tie(
        w_in, pack_near, lines, h_y, h_yc, qxf, qwg, qwf, qzg2, qzf2
    )

    other = send(lines, _zxor(1))
    other, qzg2, qzf2 = tie(other, qzg2, qzf2)
    lines = jnp.concatenate([lines, other], axis=0)
    qwg2, qxf2 = send(qwg, xm), send(qxf, xp)
    qzg3, qzf3 = send(qzg2, zm), send(qzf2, zp)
    far_a, far_b, pack_near = tie(*quantize(h_y, send(h_yc, SWAP_CORE)), pack_near)
    far_a = send(far_a, SWAP_YH)
    part, h_c = near_grad(
        fill_forward, [line_base, pack_near], spec, p_line, w_in, p_block, p, 2
    )
    part, h_c, lines, far_a, far_b, qwg2, qxf2, qzg3, qzf3 = tie(
        part, h_c, lines, far_a, far_b, qwg2, qxf2, qzg3, qzf3
    )

    pack4 = send(lines[1], SWAP_CORE)
    q_block = [q, qxf, qxg, qxf2, q_l, qwf, qwg, qwg2]
    q_bottom, q_top = send(qzg3[half:], zm), send(qzf3[:half], zp)
    q_line7 = [q, qzf1, qzg1, qzf2, qzg2, qzf3, qzg3]
    specs = [SMEM_SPEC, SMEM_SPEC, whole((8, 16, ROWS))]

    def fill(first, which):
        return functools.partial(fill_backward, first=first, which=which)

    seven = tuple(range(7))
    h_y, h_yc = hard_grad(fill(2, seven), [group_base, order, lines], specs, q_line7, 2)
    h_yc, lines1, pack4 = tie(h_yc, lines, pack4)
    h_yc = send(h_yc, SWAP_CORE)
    (h_c2,) = hard_grad(fill(1, seven), [group_base, order, lines1], specs, q_line7, 1)
    h_c, far_b = send(h_c, SWAP_CORE), send(far_b, SWAP_YH)
    pack4, h_y, h_c2, h_c, far_b, q_bottom, q_top = tie(
        pack4, h_y, h_c2, h_c, far_b, q_bottom, q_top
    )

    last = [q_top, q_bottom, send(q_top, SWAP_CORE), send(q_bottom, SWAP_CORE)]
    packs9 = jnp.concatenate([lines, pack4[None]], axis=0)
    order9 = jnp.concatenate([order, jnp.full((1,), 8, I32)])
    specs9 = [SMEM_SPEC, SMEM_SPEC, whole((9, 16, ROWS))]
    small = [group_base, order9, packs9]
    fill_last = functools.partial(fill_backward, first=2, which=(7, 8), groups=1)
    coded = last_far(fill_last, small, specs9, last, (h_y, h_yc))
    h_c2 = send(h_c2, SWAP_CORE)
    coded, far_a, lt_row, h_c2, packs9 = tie(coded, far_a, lt_row, h_c2, packs9)
    far2 = send(coded, SWAP_YH)
    far = jnp.concatenate([dequantize(far_a), dequantize(far_b)], axis=0)
    query_grad = part + h_c + far
    w_back = back_weights(p, q_block, lt_row)
    small = [group_base, order9, packs9]
    (part2,) = near_grad(
        fill(0, tuple(range(9))), small, specs9, q_line7 + last, w_back, q_block, q, 1, (h_c2,)
    )
    passage_grad = part2 + dequantize(far2)
    return loss.reshape(ROWS), query_grad, passage_grad


def solution(mesh):
    rows = P(("blk", "batch"), None)
    return jax.shard_map(
        body,
        mesh=mesh,
        in_specs=(rows, rows, rows, rows),
        out_specs=(P(("blk", "batch")), rows, rows),
        check_vma=False,
    )
```

```python
import functools

import jax
import jax.numpy as jnp
from jax import lax
from jax.experimental import pallas as pl
from jax.experimental.pallas import tpu as pltpu
from jax.sharding import PartitionSpec as P

ROWS = 128
WIDTH = 4096
HARD = 7
SCALE = WIDTH ** (-0.5)
AXES = ("blk", "batch")
VMEM_LIMIT = 12 * 1024 * 1024
F32, BF16, I32, I16 = jnp.float32, jnp.bfloat16, jnp.int32, jnp.int16


def _pairs(move):
    pairs = []
    for i in range(256):
        a, b = divmod(i, 32)
        yl, x = divmod(a, 4)
        yh, rest = divmod(b, 16)
        z, c = divmod(rest, 2)
        yl, x, yh, z, c = move(yl, x, yh, z, c)
        pairs.append((i, (yl * 4 + x) * 32 + yh * 16 + z * 2 + c))
    return pairs


def _x(d):
    return _pairs(lambda yl, x, yh, z, c: (yl, (x + d) % 4, yh, z, c))


def _z(d):
    return _pairs(lambda yl, x, yh, z, c: (yl, x, yh, (z + d) % 8, c))


def _zxor(m):
    return _pairs(lambda yl, x, yh, z, c: (yl, x, yh, z ^ m, c))


SWAP_CORE = _pairs(lambda yl, x, yh, z, c: (yl, x, yh, z, 1 - c))
SWAP_YH = _pairs(lambda yl, x, yh, z, c: (yl, x, 1 - yh, z, c))
SWAP_YL = _pairs(lambda yl, x, yh, z, c: (1 - yl, x, yh, z, c))
OFFSETS = (0, -1, 1, -2, 2, -3, 3, 4)


def send(value, pairs):
    return lax.ppermute(value, AXES, pairs)


def tie(*values):
    return lax.optimization_barrier(values)


def params(**kw):
    return pltpu.CompilerParams(vmem_limit_bytes=VMEM_LIMIT, **kw)


def cost(flops, nbytes):
    return pl.CostEstimate(flops=flops, bytes_accessed=nbytes, transcendentals=0)


def cat(refs):
    return jnp.concatenate([r[...] for r in refs], axis=0)


def nt(l, r):
    return lax.dot_general(l, r, (((1,), (1,)), ((), ())), preferred_element_type=F32)


def whole(shape):
    return pl.BlockSpec(shape, lambda k: tuple(0 for _ in shape))


SMEM_SPEC = pl.BlockSpec(memory_space=pltpu.SMEM)


def col_specs(arrays, chunk):
    return [pl.BlockSpec((a.shape[0], chunk), lambda k: (0, k)) for a in arrays]


def rows_of(arrays):
    return sum(a.shape[0] for a in arrays)


def scores(lhs, rhs, chunk=1024):
    m, n, nl = rows_of(lhs), rows_of(rhs), len(lhs)

    def kernel(*refs):
        out = refs[-1]
        d = nt(cat(refs[:nl]), cat(refs[nl:-1]))
        k = pl.program_id(0)

        @pl.when(k == 0)
        def _():
            out[...] = d

        @pl.when(k > 0)
        def _():
            out[...] += d

    return pl.pallas_call(
        kernel,
        grid=(WIDTH // chunk,),
        in_specs=col_specs(lhs + rhs, chunk),
        out_specs=whole((m, n)),
        out_shape=jax.ShapeDtypeStruct((m, n), F32),
        compiler_params=params(),
        cost_estimate=cost(2 * m * n * WIDTH, 2 * (m + n) * WIDTH + 4 * m * n),
        name="scores",
    )(*lhs, *rhs)


def hard_scores(bases, which, ids, line, group, chunk=1024):
    m, n, nl = rows_of(line), rows_of(group), len(line)
    steps = WIDTH // chunk

    def kernel(base, ids_ref, *refs):
        out, acc = refs[-2], refs[-1]
        d = nt(cat(refs[:nl]), cat(refs[nl:-2]))
        k = pl.program_id(0)

        @pl.when(k == 0)
        def _():
            acc[...] = d

        @pl.when(k > 0)
        def _():
            acc[...] += d

        @pl.when(k == steps - 1)
        def _():
            iota = lax.broadcasted_iota(I32, (ROWS, ROWS), 0)
            for g in range(n // ROWS):
                cols = slice(g * ROWS, (g + 1) * ROWS)
                idg = ids_ref[:, cols]
                sums = [jnp.zeros((1, ROWS), F32) for _ in range(HARD)]
                for i in range(m // ROWS):
                    rel = idg - base[which[i]]
                    s = acc[i * ROWS:(i + 1) * ROWS, cols]
                    for j in range(HARD):
                        hit = jnp.where(iota == rel[j:j + 1], s, 0.0)
                        sums[j] += jnp.sum(hit, axis=0, keepdims=True)
                out[:, cols] = jnp.concatenate(sums + [jnp.zeros((1, ROWS), F32)], axis=0)

    return pl.pallas_call(
        kernel,
        grid=(steps,),
        in_specs=[SMEM_SPEC, whole((8, n))] + col_specs(line + group, chunk),
        out_specs=whole((8, n)),
        out_shape=jax.ShapeDtypeStruct((8, n), F32),
        scratch_shapes=[pltpu.VMEM((m, n), F32)],
        compiler_params=params(),
        cost_estimate=cost(2 * m * n * WIDTH, 2 * (m + n) * WIDTH),
        name="hard_scores",
    )(bases, ids, *line, *group)


def softmax(st, hs, ids):
    m = st.shape[0]

    def kernel(st_ref, hs_ref, ids_ref, lt_ref, loss_ref, w_ref, pack_ref):
        s = st_ref[...] * SCALE
        real = lax.broadcasted_iota(I32, (8, ROWS), 0) < HARD
        h = jnp.where(real, hs_ref[...] * SCALE, -jnp.inf)
        t = jnp.maximum(
            jnp.max(s, axis=0, keepdims=True), jnp.max(h, axis=0, keepdims=True)
        )
        total = jnp.sum(jnp.exp(s - t), axis=0, keepdims=True) + jnp.sum(
            jnp.exp(h - t), axis=0, keepdims=True
        )
        lt = t + jnp.log(total)
        lt_ref[...] = lt
        own = s[:ROWS]
        i0 = lax.broadcasted_iota(I32, (ROWS, ROWS), 0)
        i1 = lax.broadcasted_iota(I32, (ROWS, ROWS), 1)
        loss_ref[...] = lt - jnp.sum(jnp.where(i0 == i1, own, 0.0), axis=0, keepdims=True)
        w = jnp.exp(s - lt)
        for i in range(m // ROWS):
            w_ref[:, i * ROWS:(i + 1) * ROWS] = w[i * ROWS:(i + 1) * ROWS].T.astype(BF16)
        hw = jnp.exp(h - lt).astype(BF16).astype(F32)
        pack_ref[:8] = jnp.where(real, hw, jnp.broadcast_to(lt, (8, ROWS)))
        pack_ref[8:] = ids_ref[...].astype(F32)

    row = jax.ShapeDtypeStruct((1, ROWS), F32)
    return pl.pallas_call(
        kernel,
        out_shape=[
            row,
            row,
            jax.ShapeDtypeStruct((ROWS, m), BF16),
            jax.ShapeDtypeStruct((16, ROWS), F32),
        ],
        compiler_params=params(),
        cost_estimate=cost(10 * m * ROWS, 6 * m * ROWS),
        name="softmax",
    )(st, hs, ids)


def spread_tile(pack, base):
    hw, rel = pack[:8], pack[8:].astype(I32) - base
    iota = lax.broadcasted_iota(I32, (ROWS, ROWS), 0)
    tile = jnp.zeros((ROWS, ROWS), F32)
    for j in range(HARD):
        tile = jnp.where(iota == rel[j:j + 1], hw[j:j + 1], tile)
    return tile


def fill_forward(w, line_base, packs, groups):
    for g in range(groups):
        cols = slice(g * ROWS, (g + 1) * ROWS)
        for i in range(8):
            tile = spread_tile(packs[:, cols], line_base[i])
            w[cols, i * ROWS:(i + 1) * ROWS] = tile.T.astype(BF16)


def fill_backward(w, group_base, order, packs, first, which, groups):
    for i, block in enumerate(which):
        pack = packs[order[block]]
        for g in range(groups):
            tile = spread_tile(pack, group_base[first + g])
            w[g * ROWS:(g + 1) * ROWS, i * ROWS:(i + 1) * ROWS] = tile.astype(BF16)


def hard_grad(fill, small, small_specs, line, groups, chunk=512):
    ns, nl = len(small), len(line)
    depth = rows_of(line)

    def kernel(*refs):
        sm, ln = refs[:ns], refs[ns:ns + nl]
        outs, w = refs[ns + nl:-1], refs[-1]

        @pl.when(pl.program_id(0) == 0)
        def _():
            fill(w, *sm, groups=groups)

        d = jnp.dot(w[...], cat(ln), preferred_element_type=F32)
        for g in range(groups):
            outs[g][...] = d[g * ROWS:(g + 1) * ROWS]

    out = [jax.ShapeDtypeStruct((ROWS, WIDTH), F32)] * groups
    return pl.pallas_call(
        kernel,
        grid=(WIDTH // chunk,),
        in_specs=small_specs + col_specs(line, chunk),
        out_specs=col_specs(out, chunk),
        out_shape=out,
        scratch_shapes=[pltpu.VMEM((groups * ROWS, depth), BF16)],
        compiler_params=params(),
        cost_estimate=cost(
            2 * groups * ROWS * depth * WIDTH, 2 * (depth + 2 * groups * ROWS) * WIDTH
        ),
        name="hard_grad",
    )(*small, *line)


def encode(v, out):
    top = jnp.max(jnp.abs(v), axis=1, keepdims=True)
    e = jnp.ceil(jnp.log2(jnp.maximum(top, 1e-30) / 32000.0))
    out[:, :WIDTH] = jnp.round(v * jnp.exp2(-e)).astype(I32).astype(I16)
    out[:, WIDTH:] = jnp.broadcast_to(e, (v.shape[0], 128)).astype(I32).astype(I16)


def last_far(fill, small, small_specs, line, before, chunk=512):
    ns, nl = len(small), len(line)
    depth = rows_of(line)
    steps = WIDTH // chunk

    def kernel(*refs):
        sm, ln = refs[:ns], refs[ns:ns + nl]
        b0, b1, out, w, total = refs[ns + nl:]
        k = pl.program_id(0)

        @pl.when(k == 0)
        def _():
            fill(w, *sm)

        d = jnp.dot(w[...], cat(ln), preferred_element_type=F32)
        cols = pl.ds(pl.multiple_of(k * chunk, chunk), chunk)
        total[:, cols] = d + b0[...] + b1[...]

        @pl.when(k == steps - 1)
        def _():
            encode(total[...], out)

    return pl.pallas_call(
        kernel,
        grid=(steps,),
        in_specs=small_specs + col_specs(line, chunk) + col_specs(list(before), chunk),
        out_specs=whole((ROWS, WIDTH + 128)),
        out_shape=jax.ShapeDtypeStruct((ROWS, WIDTH + 128), I16),
        scratch_shapes=[pltpu.VMEM((ROWS, depth), BF16), pltpu.VMEM((ROWS, WIDTH), F32)],
        compiler_params=params(),
        cost_estimate=cost(2 * ROWS * depth * WIDTH, 2 * (depth + 5 * ROWS) * WIDTH),
        name="last_far",
    )(*small, *line, *before)


def near_grad(fill, small, small_specs, line, w_in, block, minus, groups, came=(), chunk=512):
    ns, nl, nb, nc = len(small), len(line), len(block), len(came)
    depth = rows_of(line)

    def kernel(*refs):
        sm, ln = refs[:ns], refs[ns:ns + nl]
        w_ref, bl = refs[ns + nl], refs[ns + nl + 1:ns + nl + 1 + nb]
        minus_ref, *rest = refs[ns + nl + 1 + nb:]
        cm, outs, w = rest[:nc], rest[nc:-1], rest[-1]

        @pl.when(pl.program_id(0) == 0)
        def _():
            fill(w, *sm, groups=groups)

        d = jnp.dot(w[...], cat(ln), preferred_element_type=F32)
        e = jnp.dot(w_ref[...], cat(bl), preferred_element_type=F32)
        own = d[:ROWS] + e - minus_ref[...].astype(F32)
        for c in cm:
            own += c[...]
        outs[0][...] = own
        for g in range(1, groups):
            outs[g][...] = d[g * ROWS:(g + 1) * ROWS]

    out = [jax.ShapeDtypeStruct((ROWS, WIDTH), F32)] * groups
    return pl.pallas_call(
        kernel,
        grid=(WIDTH // chunk,),
        in_specs=small_specs
        + col_specs(line, chunk)
        + [whole(w_in.shape)]
        + col_specs(block + [minus] + list(came), chunk),
        out_specs=col_specs(out, chunk),
        out_shape=out,
        scratch_shapes=[pltpu.VMEM((groups * ROWS, depth), BF16)],
        compiler_params=params(),
        cost_estimate=cost(6 * ROWS * 8 * ROWS * WIDTH, 22 * ROWS * 2 * WIDTH),
        name="near_grad",
    )(*small, *line, w_in, *block, minus, *came)


def quantize(a, b):
    half = ROWS // 2

    def kernel(a_ref, b_ref, out0, out1):
        encode(a_ref[:half] + b_ref[:half], out0)
        encode(a_ref[half:] + b_ref[half:], out1)

    out = jax.ShapeDtypeStruct((half, WIDTH + 128), I16)
    return pl.pallas_call(
        kernel,
        out_shape=[out, out],
        compiler_params=params(),
        cost_estimate=cost(6 * ROWS * WIDTH, 10 * ROWS * WIDTH),
        name="quantize",
    )(a, b)


def dequantize(coded):
    step = jnp.exp2(coded[:, WIDTH:WIDTH + 1].astype(F32))
    return coded[:, :WIDTH].astype(F32) * step


def back_weights(p, block, lt_row, chunk=1024):
    nb = len(block)
    n = rows_of(block)
    steps = WIDTH // chunk

    def kernel(p_ref, lt_ref, *refs):
        out, acc = refs[-2], refs[-1]
        d = nt(p_ref[...], cat(refs[:nb]))
        k = pl.program_id(0)

        @pl.when(k == 0)
        def _():
            acc[...] = d

        @pl.when(k > 0)
        def _():
            acc[...] += d

        @pl.when(k == steps - 1)
        def _():
            out[...] = jnp.exp(acc[...] * SCALE - lt_ref[...]).astype(BF16)

    return pl.pallas_call(
        kernel,
        grid=(steps,),
        in_specs=col_specs([p], chunk) + [whole((1, n))] + col_specs(block, chunk),
        out_specs=whole((ROWS, n)),
        out_shape=jax.ShapeDtypeStruct((ROWS, n), BF16),
        scratch_shapes=[pltpu.VMEM((ROWS, n), F32)],
        compiler_params=params(),
        cost_estimate=cost(2 * ROWS * n * WIDTH, 2 * (ROWS + n) * WIDTH),
        name="back_weights",
    )(p, lt_row, *block)


def body(q, p, hard_owner, hard_row):
    b = lax.axis_index("batch").astype(I32)
    z = (b // 2) % 8
    line_z = (z + jnp.array(OFFSETS, I32)) % 8
    step = z ^ line_z
    order = (step & 1) + (step // 4) * 2 + (step & 2) * 2
    line_base = ((b // 16) * 16 + line_z * 2 + b % 2) * ROWS
    group_base = (b ^ jnp.array([0, 1, 16, 17], I32)) * ROWS
    half = ROWS // 2
    xp, xm, zp, zm = _x(1), _x(-1), _z(1), _z(-1)

    ids = (hard_owner * ROWS + hard_row).T
    ids = jnp.concatenate([ids, jnp.full((1, ROWS), -1, I32)], axis=0)

    q_c, ids_c = send(q, SWAP_CORE), send(ids, SWAP_CORE)
    q_c, ids_c, p1 = tie(q_c, ids_c, p)
    zg1, zf1 = send(p1, zm), send(p1, zp)
    xg, xf, w = send(p, xm), send(p, xp), send(p, SWAP_YL)
    w, q_c, ids_c, q1 = tie(w, q_c, ids_c, q)
    zg2, zf2 = send(zg1, zm), send(zf1, zp)
    w1, xf1, xg, xf = tie(w, xf, xg, xf)
    wg, wf = send(w1, xm), send(w1, xp)
    q_y = send(q1, SWAP_YH)
    ids_near = jnp.concatenate([ids, ids_c], axis=1)
    q_y, ids_near, q1 = tie(q_y, ids_near, q1)
    ids_far = send(ids_near, SWAP_YH)
    ids_far, q2 = tie(ids_far, q1)
    wg, wf, xf1 = tie(wg, wf, xf1)
    zg3, zf3 = send(zg2, zm), send(zf2, zp)
    q_yc, q_l, wg2, xf2 = send(q_y, SWAP_CORE), send(q2, SWAP_YL), send(wg, xm), send(xf1, xp)
    q_group = [q, q_c, q_y, q_yc]
    ids_group = jnp.concatenate([ids_near, ids_far], axis=1)
    near5 = [p, zf1, zg1, zf2, zg2]
    hs = hard_scores(line_base, (0, 1, 2, 3, 4), ids_group, near5, q_group)
    q3, hs, wg2, xf2, zg3, zf3 = tie(q2, hs, wg2, xf2, zg3, zf3)

    qxg, qxf = send(q3, xm), send(q3, xp)
    bottom, top = send(zg3[half:], zm), send(zf3[:half], zp)
    p_block = [p, xf, xg, xf2, w, wf, wg, wg2]
    hs = hs + hard_scores(line_base, (5, 6), ids_group, [zf3, zg3], q_group)
    st = scores(p_block, [q])
    q4, hs, st, q_l, bottom, top = tie(q3, hs, st, q_l, bottom, top)

    qzg1, qzf1 = send(q4, zm), send(q4, zp)
    hs = hs + hard_scores(line_base, (7,), ids_group, [top, bottom], q_group)
    hs = hs.reshape(8, 2, 2, ROWS)
    mine = hs[:, :, 0] + send(hs[:, :, 1], SWAP_CORE)
    hs = mine[:, 0] + send(mine[:, 1], SWAP_YH)
    hs, qxg, qxf = tie(hs, qxg, qxf)
    lt, loss, w_in, pack = softmax(st, hs, ids)
    lt2 = jnp.concatenate([lt, send(lt, SWAP_YL)], axis=0)
    pack_near = jnp.concatenate([pack, send(pack, SWAP_CORE)], axis=1)
    pack_far = send(pack_near, SWAP_YH)
    lt_2, lt_g, lt_f = send(lt2, _x(2)), send(lt2, xm), send(lt2, xp)
    lt_row = jnp.stack([lt2, lt_f, lt_g, lt_2], axis=1).reshape(1, 8 * ROWS)
    pack, pack_far, lt_row = tie(pack, pack_far, lt_row)
    other = send(pack[None], _zxor(1))
    lines = jnp.concatenate([pack[None], other], axis=0)
    pack_near, pack_far, lines, lt_row, q_l, qxg, qxf, qzg1, qzf1 = tie(
        pack_near, pack_far, lines, lt_row, q_l, qxg, qxf, qzg1, qzf1
    )

    other = send(lines, _zxor(4))
    lines = jnp.concatenate([lines, other], axis=0)
    qwg, qwf = send(q_l, xm), send(q_l, xp)
    qzg2, qzf2 = send(qzg1, zm), send(qzf1, zp)
    p_line = [p, zf1, zg1, zf2, zg2, zf3, zg3, top, bottom]
    spec = [SMEM_SPEC, whole((16, 2 * ROWS))]
    h_y, h_yc = hard_grad(fill_forward, [line_base, pack_far], spec, p_line, 2)
    w_in, pack_near, lines, h_y, h_yc, qxf, qwg, qwf, qzg2, qzf2 = tie(
        w_in, pack_near, lines, h_y, h_yc, qxf, qwg, qwf, qzg2, qzf2
    )

    other = send(lines, _zxor(2))
    other, qzg2, qzf2 = tie(other, qzg2, qzf2)
    lines = jnp.concatenate([lines, other], axis=0)
    qwg2, qxf2 = send(qwg, xm), send(qxf, xp)
    qzg3, qzf3 = send(qzg2, zm), send(qzf2, zp)
    far_a, far_b, pack_near = tie(*quantize(h_y, send(h_yc, SWAP_CORE)), pack_near)
    far_a = send(far_a, SWAP_YH)
    part, h_c = near_grad(
        fill_forward, [line_base, pack_near], spec, p_line, w_in, p_block, p, 2
    )
    part, h_c, lines, far_a, far_b, qwg2, qxf2, qzg3, qzf3 = tie(
        part, h_c, lines, far_a, far_b, qwg2, qxf2, qzg3, qzf3
    )

    pack4 = send(lines[2], SWAP_CORE)
    q_block = [q, qxf, qxg, qxf2, q_l, qwf, qwg, qwg2]
    q_bottom, q_top = send(qzg3[half:], zm), send(qzf3[:half], zp)
    q_line7 = [q, qzf1, qzg1, qzf2, qzg2, qzf3, qzg3]
    specs = [SMEM_SPEC, SMEM_SPEC, whole((8, 16, ROWS))]

    def fill(first, which):
        return functools.partial(fill_backward, first=first, which=which)

    seven = tuple(range(7))
    h_y, h_yc = hard_grad(fill(2, seven), [group_base, order, lines], specs, q_line7, 2)
    h_yc, lines1, pack4 = tie(h_yc, lines, pack4)
    h_yc = send(h_yc, SWAP_CORE)
    (h_c2,) = hard_grad(fill(1, seven), [group_base, order, lines1], specs, q_line7, 1)
    h_c, far_b = send(h_c, SWAP_CORE), send(far_b, SWAP_YH)
    pack4, h_y, h_c2, h_c, far_b, q_bottom, q_top = tie(
        pack4, h_y, h_c2, h_c, far_b, q_bottom, q_top
    )

    last = [q_top, q_bottom, send(q_top, SWAP_CORE), send(q_bottom, SWAP_CORE)]
    packs9 = jnp.concatenate([lines, pack4[None]], axis=0)
    order9 = jnp.concatenate([order, jnp.full((1,), 8, I32)])
    specs9 = [SMEM_SPEC, SMEM_SPEC, whole((9, 16, ROWS))]
    small = [group_base, order9, packs9]
    fill_last = functools.partial(fill_backward, first=2, which=(7, 8), groups=1)
    coded = last_far(fill_last, small, specs9, last, (h_y, h_yc))
    h_c2 = send(h_c2, SWAP_CORE)
    coded, far_a, lt_row, h_c2, packs9 = tie(coded, far_a, lt_row, h_c2, packs9)
    far2 = send(coded, SWAP_YH)
    far = jnp.concatenate([dequantize(far_a), dequantize(far_b)], axis=0)
    query_grad = part + h_c + far
    w_back = back_weights(p, q_block, lt_row)
    small = [group_base, order9, packs9]
    (part2,) = near_grad(
        fill(0, tuple(range(9))), small, specs9, q_line7 + last, w_back, q_block, q, 1, (h_c2,)
    )
    passage_grad = part2 + dequantize(far2)
    return loss.reshape(ROWS), query_grad, passage_grad


def solution(mesh):
    rows = P(("blk", "batch"), None)
    return jax.shard_map(
        body,
        mesh=mesh,
        in_specs=(rows, rows, rows, rows),
        out_specs=(P(("blk", "batch")), rows, rows),
        check_vma=False,
    )
```
